32 devices in a mesh: lat: 4 (over y, x), lon: 8 (over z, core).
Axes of the slice: x: 2, y: 2, z: 4, core: 2. Of those that a mesh axis runs over, the one named last changes fastest.
Arguments:
- ensemble: float32 [16, 64, 1792], P('lat', 'lon'), may hold values from -6 to 6
- northward_wind: float32 [16, 64], P('lat', 'lon'), may hold values from -1 to 1
- eastward_wind: float32 [16, 64], P('lat', 'lon'), may hold values from -1 to 1
- spreading_strength: float32 [16, 64], P('lat', 'lon'), may hold values from 0.05 to 0.2
- measurement_home_subdomain: int32 [3, 128], replicated, may hold values from 0 to 31, as said below
- obs_site: int32 [3, 128], replicated, may hold values from 0 to 895
- obs_class: int32 [3, 128], replicated, may hold values from 0 to 7
- cutoff_table: int32 [8], replicated, may hold values from 6 to 23
- obs_value: float32 [3, 128], replicated, may hold values from -6 to 6
- obs_var: float32 [3, 128], replicated, may hold values from 0.5 to 2
- obs_noise: float32 [3, 128, 64], replicated, may hold values from -6 to 6
Outputs:
- analysis: float32 [16, 64, 1792], P('lat', 'lon')
The draws below stay inside these ranges and needn't reach their ends.
Inputs may be any that keep to these rules, and one draw needn't show every extreme that they name: `measurement_home_subdomain`: tile index is lat index * 8 + lon index; in every batch no tile owns more than 4 observations and some tile owns exactly 4.
All inputs are finite; a program needn't handle non-finite values.
Results may differ from the reference program's by a relative error of at most 0.0003.
Values sent between devices are 32-bit elements; how exact they have to be, the bound alone decides.
A program may use at most 64 MiB of HBM per device.

```python
import math
import jax
import jax.numpy as jnp
from jax import lax

CLAT = 4
CLON = 8
LEV = 28
MEMBERS = 64
SECTIONS = 2
BATCH_GROUPS = 3
CAP = 4
CLASSES = 8
NB = 128
NLAT = 16
NLON = 64
CELLS = 32
N_LAT = 4
N_LON = 8


def draw_measurement_home_subdomain(key, part):
    tiles = N_LAT * N_LON
    batches = []
    for b in range(BATCH_GROUPS):
        sub = jax.random.fold_in(key, b + 11)
        order_tiles = jax.random.permutation(jax.random.fold_in(sub, 1), tiles).astype(jnp.int32)
        hot = order_tiles[tiles - 1]
        rest = order_tiles[jnp.arange(NB - CAP, dtype=jnp.int32) % (tiles - 1)]
        listed = jnp.concatenate([jnp.full((CAP,), hot, jnp.int32), rest])
        shuffle_order = jax.random.permutation(jax.random.fold_in(sub, 2), NB).astype(jnp.int32)
        batches.append(listed[shuffle_order])
    return jnp.stack(batches).astype(jnp.int32)


def with_ends(drawn, stream_key, smallest, largest):
    extent = drawn.shape
    index_at = [jax.random.randint(jax.random.fold_in(stream_key, axis), (), 0, extent[axis]) for axis in range(len(extent))]
    drawn = drawn.at[tuple(index_at)].set(smallest)
    longest = extent.index(max(extent))
    index_at[longest] = (index_at[longest] + 1) % extent[longest]
    return drawn.at[tuple(index_at)].set(largest)


def block_scale(rng, dims, cuts, smallest, largest):
    factor_of, own = 1.0, jax.random.fold_in(rng, 6)
    for dim, parts in cuts:
        draws = jnp.exp(jax.random.uniform(jax.random.fold_in(own, dim), (parts,), jnp.float32, smallest / len(cuts), largest / len(cuts)))
        factor_of = factor_of * jnp.repeat(draws, dims[dim] // parts).reshape([-1 if axis == dim else 1 for axis in range(len(dims))])
    return factor_of


def centred(key, dims, width, reach, pieces=(), kind=jnp.bfloat16):
    array = width * jax.random.normal(key, dims, jnp.float32)
    if pieces:
        array = array * block_scale(key, dims, pieces, -0.22, 0.18)
    return jnp.clip(array, -reach, reach).astype(kind)


def setup_inputs(seed: int = 0) -> dict:
    key_list = jax.random.split(jax.random.key(seed), 12)
    ensemble = centred(key_list[0], (NLAT, NLON, LEV * MEMBERS), 1.0, 6.0, ((0, 4), (1, 8)), jnp.float32)
    northward_wind = jnp.clip(jax.random.uniform(key_list[1], (NLAT, NLON), jnp.float32, -1.0, 1.0) * block_scale(key_list[1], (NLAT, NLON), ((0, 4), (1, 8)), -0.4, 0.0), -1.0, 1.0)
    eastward_wind = jnp.clip(jax.random.uniform(key_list[2], (NLAT, NLON), jnp.float32, -1.0, 1.0) * block_scale(key_list[2], (NLAT, NLON), ((0, 4), (1, 8)), -0.4, 0.0), -1.0, 1.0)
    spreading_strength = jnp.clip(jnp.exp(math.log(0.2) - 1.3862944 * jax.random.uniform(key_list[3], (NLAT, NLON), jnp.float32) ** block_scale(key_list[3], (NLAT, NLON), ((0, 4), (1, 8)), -0.2, 0.2)), 0.05, 0.2)
    measurement_home_subdomain = draw_measurement_home_subdomain(jax.random.fold_in(key_list[11], 71), 0)
    obs_site = with_ends(jax.random.randint(key_list[5], (BATCH_GROUPS, NB), 0, CELLS * LEV), jax.random.fold_in(key_list[5], 1), 0, (CELLS * LEV) - 1).astype(jnp.int32)
    obs_class = with_ends(jax.random.randint(key_list[6], (BATCH_GROUPS, NB), 0, CLASSES), jax.random.fold_in(key_list[6], 1), 0, CLASSES - 1).astype(jnp.int32)
    cutoff_table = with_ends(jax.random.randint(key_list[7], (CLASSES,), 6, 24), jax.random.fold_in(key_list[7], 1), 6, 23).astype(jnp.int32)
    obs_value = centred(key_list[8], (BATCH_GROUPS, NB), 1.0, 6.0, (), jnp.float32)
    obs_var = jnp.clip(jnp.exp(jax.random.uniform(key_list[9], (BATCH_GROUPS, NB), jnp.float32, math.log(0.5), math.log(2.0))), 0.5, 2.0)
    obs_noise = centred(key_list[10], (BATCH_GROUPS, NB, MEMBERS), 1.0, 6.0, (), jnp.float32)
    return dict(ensemble=ensemble, northward_wind=northward_wind, eastward_wind=eastward_wind, spreading_strength=spreading_strength, measurement_home_subdomain=measurement_home_subdomain, obs_site=obs_site, obs_class=obs_class, cutoff_table=cutoff_table, obs_value=obs_value, obs_var=obs_var, obs_noise=obs_noise)


advect_coef = 0.2

def taper(dist, radius):
    z = dist / radius
    inner = 1.0 - 5.0 / 3.0 * z ** 2 + 0.625 * z ** 3 + 0.5 * z ** 4 - 0.25 * z ** 5
    outside = jnp.maximum(z, 1.0)
    outer = 4.0 - 5.0 * outside + 5.0 / 3.0 * outside ** 2 + 0.625 * outside ** 3 - 0.5 * outside ** 4 + outside ** 5 / 12.0 - 2.0 / (3.0 * outside)
    return jnp.where(z <= 1.0, inner, jnp.where(z < 2.0, outer, jnp.float32(0.0)))

def advance_subdomains(prognostic_fields, northward_wind, eastward_wind, spreading_strength):
    padded = jnp.pad(prognostic_fields, ((1, 1), (0, 0), (0, 0)))
    north = padded[2:]
    south = padded[:-2]
    east = jnp.roll(prognostic_fields, -1, axis=1)
    west = jnp.roll(prognostic_fields, 1, axis=1)
    lap = north + south + east + west - 4.0 * prognostic_fields
    return prognostic_fields + spreading_strength[:, :, None] * lap - advect_coef * (northward_wind[:, :, None] * (north - south) + eastward_wind[:, :, None] * (east - west))

def whiten(prior, value, var, noise):
    mean = lax.optimization_barrier(jnp.mean(prior, axis=1, keepdims=True))
    anom = prior - mean
    cov = jnp.dot(anom, anom.T, precision=lax.Precision.HIGHEST) / jnp.float32(MEMBERS - 1) + jnp.diag(var)
    factor = jnp.linalg.cholesky(cov)
    rhs = value[:, None] + jnp.sqrt(var)[:, None] * noise - prior
    return (anom, jax.scipy.linalg.cho_solve((factor, True), rhs))

def reference(ensemble, northward_wind, eastward_wind, spreading_strength, measurement_home_subdomain, obs_site, obs_class, cutoff_table, obs_value, obs_var, obs_noise):
    prognostic_fields = ensemble
    for section in range(SECTIONS):
        prognostic_fields = advance_subdomains(prognostic_fields, northward_wind, eastward_wind, spreading_strength)
    for k in range(BATCH_GROUPS):
        owner = measurement_home_subdomain[k].astype(jnp.int32)
        site = obs_site[k].astype(jnp.int32)
        cell = site // LEV
        level = site % LEV
        glat = owner // N_LON * CLAT + cell // CLON
        glon = owner % N_LON * CLON + cell % CLON
        grid = prognostic_fields.reshape(NLAT, NLON, LEV, MEMBERS)
        prior = grid[glat, glon, level]
        anom_obs, white = whiten(prior, obs_value[k], obs_var[k], obs_noise[k])
        radius = cutoff_table[obs_class[k]].astype(jnp.float32)
        vertical_profiles = jnp.arange(NLON, dtype=jnp.int32)

        def update(args):
            xrow, ilat = args
            dlat = jnp.abs(ilat - glat).astype(jnp.float32)
            dlon = jnp.abs(vertical_profiles[:, None] - glon[None, :])
            dlon = jnp.minimum(dlon, NLON - dlon).astype(jnp.float32)
            dist = jnp.sqrt(dlat[None, :] * dlat[None, :] + dlon * dlon)
            rho = taper(dist, radius[None, :])
            cube = xrow.reshape(NLON, LEV, MEMBERS)
            xp = cube - lax.optimization_barrier(jnp.mean(cube, axis=2, keepdims=True))
            cov = jnp.einsum('clm,jm->clj', xp, anom_obs, precision=lax.Precision.HIGHEST) / jnp.float32(MEMBERS - 1)
            inc = jnp.einsum('clj,jm->clm', cov * rho[:, None, :], white, precision=lax.Precision.HIGHEST)
            return (cube + inc).reshape(NLON, LEV * MEMBERS)
        prognostic_fields = lax.map(update, (prognostic_fields, jnp.arange(NLAT, dtype=jnp.int32)))
    return prognostic_fields
```

```python
import functools

import jax
import jax.numpy as jnp
from jax import lax
from jax.experimental import pallas as pl
from jax.experimental.pallas import tpu as pltpu
from jax.sharding import PartitionSpec as P

LEV = 28
MEMBERS = 64
SECTIONS = 2
BATCH_GROUPS = 3
CAP = 4
LANES = 128
PIVOTS = 4

advect_coef = 0.2
MESH = pl.DeviceIdType.MESH
HIGHEST = lax.Precision.HIGHEST
SLOT_ROWS = -(-(BATCH_GROUPS * CAP) // 16) * 8


def floor_div(value, divisor):
    return jnp.floor((value + 0.5) * (1.0 / divisor))


def dot_t(a, b, precision=None):
    return lax.dot_general(
        a, b, (((1,), (1,)), ((), ())), precision=precision, preferred_element_type=jnp.float32
    )


def dot_n(a, b, precision=None):
    return lax.dot_general(
        a, b, (((1,), (0,)), ((), ())), precision=precision, preferred_element_type=jnp.float32
    )


def split(value):
    high = value.astype(jnp.bfloat16)
    low = (value - high.astype(jnp.float32)).astype(jnp.bfloat16)
    return high, low


def iota(shape, dim):
    return lax.broadcasted_iota(jnp.int32, shape, dim)


def column(row):
    n = row.shape[1]
    return jnp.sum(
        jnp.where(iota((n, n), 0) == iota((n, n), 1), row, 0.0), axis=1, keepdims=True
    )


def forecast_kernel(
    lat_n,
    lon_n,
    ens_ref,
    north_ref,
    east_ref,
    spread_ref,
    owner_ref,
    site_ref,
    state_ref,
    gather_ref,
    rank_ref,
    mid,
    edge,
    halo_lat,
    halo_lon,
    slots,
    send_sem,
    recv_sem,
    lon_send,
    lon_recv,
    lat_send,
    lat_recv,
):
    ilat = lax.axis_index("lat")
    ilon = lax.axis_index("lon")
    tile_lat, tile_lon, width = ens_ref.shape
    pairs = width // LANES
    lon_peers = [lax.rem(ilon + d, lon_n) for d in range(1, lon_n)]
    lat_peers = [lax.rem(ilat + d, lat_n) for d in range(1, lat_n)]

    barrier = pltpu.get_barrier_semaphore()
    for peer in lon_peers:
        pl.semaphore_signal(barrier, inc=1, device_id=(ilat, peer), device_id_type=MESH)
    for peer in lat_peers:
        pl.semaphore_signal(barrier, inc=1, device_id=(peer, ilon), device_id_type=MESH)

    def fill_edges(section, src):
        for i in range(tile_lat):
            edge[section, 0, i : i + 1, :] = src[i, tile_lon - 1 : tile_lon, :]
            edge[section, 1, i : i + 1, :] = src[i, 0:1, :]

    def start(section, src):
        up = lax.rem(ilat + 1, lat_n)
        down = lax.rem(ilat + lat_n - 1, lat_n)
        right = lax.rem(ilon + 1, lon_n)
        left = lax.rem(ilon + lon_n - 1, lon_n)
        moves = (
            (src.at[tile_lat - 1], halo_lat.at[section, 0], (up, ilon)),
            (src.at[0], halo_lat.at[section, 1], (down, ilon)),
            (edge.at[section, 0], halo_lon.at[section, 0], (ilat, right)),
            (edge.at[section, 1], halo_lon.at[section, 1], (ilat, left)),
        )
        copies = []
        for n, (a, b, device) in enumerate(moves):
            copy = pltpu.make_async_remote_copy(
                src_ref=a,
                dst_ref=b,
                send_sem=send_sem.at[section, n],
                recv_sem=recv_sem.at[section, n],
                device_id=device,
                device_id_type=MESH,
            )
            copy.start()
            copies.append(copy)
        return copies

    fill_edges(0, ens_ref)
    pl.semaphore_wait(barrier, len(lon_peers) + len(lat_peers))
    copies = start(0, ens_ref)

    same = iota((tile_lon, tile_lon), 0) == iota((tile_lon, tile_lon), 1)
    coef = []
    for i in range(tile_lat):
        s, n, e = (
            jnp.sum(jnp.where(same, ref[i : i + 1, :], 0.0), axis=1, keepdims=True)
            for ref in (spread_ref, north_ref, east_ref)
        )
        n = advect_coef * n
        e = advect_coef * e
        coef.append((1.0 - 4.0 * s, s - n, s + n, s - e, s + e))

    count = owner_ref.shape[1]
    me = (ilat * lon_n + ilon).astype(jnp.float32)
    half = SLOT_ROWS
    slot_iota = iota((2 * half, count), 0)
    slot_id = (2 * (slot_iota % half) + slot_iota // half).astype(jnp.float32)
    slot_row = jnp.zeros((2 * half, 1), jnp.float32)
    slot_odd = jnp.zeros((2 * half, 1), jnp.float32)
    rank_ref[...] = jnp.zeros(rank_ref.shape, jnp.float32)
    for k in range(BATCH_GROUPS):
        owner = owner_ref[k : k + 1, :].astype(jnp.float32)
        site = site_ref[k : k + 1, :].astype(jnp.float32)
        before = iota((count, count), 0) < iota((count, count), 1)
        earlier = (column(owner) == owner) & before
        rank = jnp.sum(jnp.where(earlier, 1.0, 0.0), axis=0, keepdims=True)
        rank_ref[k : k + 1, :] = rank
        cell = floor_div(site, LEV)
        level = site - LEV * cell
        cell_lat = floor_div(cell, tile_lon)
        cell_lon = cell - tile_lon * cell_lat
        pair = floor_div(level, 2)
        row = (cell_lat * pairs + pair) * tile_lon + cell_lon
        mine = (owner == me) & (slot_id == rank + float(CAP * k))
        slot_row += jnp.sum(jnp.where(mine, row, 0.0), axis=1, keepdims=True)
        slot_odd += jnp.sum(jnp.where(mine, level - 2.0 * pair, 0.0), axis=1, keepdims=True)
    rows = tile_lat * width // LANES * tile_lon
    pick = jnp.where(
        iota((2 * half, rows), 1).astype(jnp.float32) == slot_row, 1.0, 0.0
    )

    src = ens_ref
    for section in range(SECTIONS):
        for copy in copies:
            copy.wait()
        last = section == SECTIONS - 1
        for i in range(tile_lat):
            centre, c_n, c_s, c_e, c_w = coef[i]
            here = src[i]
            if i + 1 < tile_lat:
                above = src[i + 1]
            else:
                above = jnp.where(ilat == lat_n - 1, 0.0, halo_lat[section, 1])
            if i > 0:
                below = src[i - 1]
            else:
                below = jnp.where(ilat == 0, 0.0, halo_lat[section, 0])
            east = jnp.concatenate([here[1:], halo_lon[section, 1, i : i + 1, :]], axis=0)
            west = jnp.concatenate([halo_lon[section, 0, i : i + 1, :], here[:-1]], axis=0)
            new = centre * here + c_n * above + c_s * below + c_e * east + c_w * west
            if last:
                for p in range(pairs):
                    at = (i * pairs + p) * tile_lon
                    state_ref[at : at + tile_lon, :] = new[:, p * LANES : (p + 1) * LANES]
            else:
                mid[section, i] = new
        if not last:
            src = mid.at[section]
            fill_edges(section + 1, src)
            copies = start(section + 1, src)

    taken = dot_n(pick, state_ref[...], HIGHEST)
    first, second = taken[:half], taken[half:]
    first = jnp.where(slot_odd[:half] < 0.5, first, pltpu.roll(first, MEMBERS, 1))
    second = jnp.where(slot_odd[half:] > 0.5, second, pltpu.roll(second, MEMBERS, 1))
    low_half = iota((half, LANES), 1) < MEMBERS
    slots[ilat, ilon] = jnp.where(low_half, first, second)

    def share(src_at, peers, sends, recvs, device_of):
        out = []
        for n, peer in enumerate(peers):
            copy = pltpu.make_async_remote_copy(
                src_ref=src_at,
                dst_ref=src_at,
                send_sem=sends.at[n],
                recv_sem=recvs.at[n],
                device_id=device_of(peer),
                device_id_type=MESH,
            )
            copy.start()
            out.append(copy)
        for copy in out:
            copy.wait()

    share(slots.at[ilat, ilon], lon_peers, lon_send, lon_recv, lambda peer: (ilat, peer))
    share(slots.at[ilat], lat_peers, lat_send, lat_recv, lambda peer: (peer, ilon))
    gather_ref[...] = slots[...].reshape(gather_ref.shape)


def taper(dist, inverse_radius):
    z = dist * inverse_radius
    inner = 1.0 + z * z * (-5.0 / 3.0 + z * (0.625 + z * (0.5 - 0.25 * z)))
    o = jnp.maximum(z, 1.0)
    outer = (
        4.0
        + o * (-5.0 + o * (5.0 / 3.0 + o * (0.625 + o * (-0.5 + o * (1.0 / 12.0)))))
        - (2.0 / 3.0) / o
    )
    return jnp.where(z <= 1.0, inner, jnp.where(z < 2.0, outer, 0.0))


def gauss_jordan(aug):
    size = aug.shape[0]
    blocks = [aug[i : i + 8] for i in range(0, size, 8)]
    sub = iota((8, LANES), 0)
    for base in range(0, size, PIVOTS):
        home, at = base // 8, base % 8
        cols = [
            [jnp.broadcast_to(block[:, base + j : base + j + 1], (8, LANES)) for block in blocks]
            for j in range(PIVOTS)
        ]
        rows = [blocks[home][at + i : at + i + 1] for i in range(PIVOTS)]
        c = [[cols[j][home][at + i : at + i + 1] for j in range(PIVOTS)] for i in range(PIVOTS)]
        for i in range(PIVOTS):
            inverse = 1.0 / c[i][i]
            rows[i] = rows[i] * inverse
            for j in range(i + 1, PIVOTS):
                c[i][j] = c[i][j] * inverse
            for r in range(PIVOTS):
                if r != i:
                    f = c[r][i]
                    rows[r] = rows[r] - f * rows[i]
                    for j in range(i + 1, PIVOTS):
                        c[r][j] = c[r][j] - f * c[i][j]
        wide = [jnp.broadcast_to(row, (8, LANES)) for row in rows]
        for b in range(len(blocks)):
            new = blocks[b]
            for j in range(PIVOTS):
                new = new - cols[j][b] * wide[j]
            if b == home:
                for j in range(PIVOTS):
                    new = jnp.where(sub == at + j, wide[j], new)
            blocks[b] = new
    return jnp.concatenate(blocks, axis=0)


def update_kernel(
    lat_n,
    lon_n,
    state_ref,
    gather_ref,
    rank_ref,
    owner_ref,
    site_ref,
    class_ref,
    cutoff_ref,
    value_ref,
    var_ref,
    noise_ref,
    out_ref,
    x_ref,
    noise_wide,
):
    tile_lat, tile_lon, width = out_ref.shape
    pairs = width // LANES
    ilat = lax.axis_index("lat")
    ilon = lax.axis_index("lon")
    lon_cells = float(tile_lon * lon_n)
    count = owner_ref.shape[1]
    scale = 1.0 / (MEMBERS - 1)
    low_lanes = iota((count, LANES), 1) < MEMBERS

    rows_of = []
    stacked = []
    for k in range(BATCH_GROUPS):
        owner = owner_ref[k : k + 1, :].astype(jnp.float32)
        site = site_ref[k : k + 1, :].astype(jnp.float32)
        classes = class_ref[k : k + 1, :]
        cell = floor_div(site, LEV)
        cell_lat = floor_div(cell, tile_lon)
        tile_row = floor_div(owner, lon_n)
        glat = tile_row * tile_lat + cell_lat
        glon = (owner - lon_n * tile_row) * tile_lon + cell - tile_lon * cell_lat
        radius = jnp.zeros((1, count), jnp.float32)
        for c in range(cutoff_ref.shape[0]):
            radius = jnp.where(classes == c, cutoff_ref[c].astype(jnp.float32), radius)
        slot = rank_ref[k : k + 1, :] + float(CAP * k)
        slot_half = floor_div(slot, 2)
        rows_of.append((glat, glon, 1.0 / radius))
        stacked += [
            glat,
            glon,
            owner * SLOT_ROWS + slot_half,
            slot - 2.0 * slot_half,
            value_ref[k : k + 1, :],
            var_ref[k : k + 1, :],
            jnp.zeros((2, count), jnp.float32),
        ]
    table = jnp.concatenate(stacked, axis=0).T

    def col(k, n):
        return table[:, 8 * k + n : 8 * k + n + 1]

    def rho_of(lat_at, lon_at, k):
        glat, glon, inverse_radius = rows_of[k]
        dlat = jnp.abs(lat_at - glat)
        dlon = jnp.abs(lon_at - glon)
        dlon = jnp.minimum(dlon, lon_cells - dlon)
        return scale * taper(jnp.sqrt(dlat * dlat + dlon * dlon), inverse_radius)

    slots = gather_ref.shape[0]
    priors = []
    for k in range(BATCH_GROUPS):
        pick = jnp.where(iota((count, slots), 1).astype(jnp.float32) == col(k, 2), 1.0, 0.0)
        taken = dot_n(pick, gather_ref[...], HIGHEST)
        turned = pltpu.roll(taken, MEMBERS, 1)
        odd = col(k, 3) > 0.5
        priors.append(jnp.where(odd != low_lanes, taken, turned))

    for k in range(BATCH_GROUPS):
        prior = priors[k]
        var = col(k, 5)
        inverse_var = 1.0 / var
        anom = prior - jnp.mean(prior, axis=1, keepdims=True)
        noise_wide[:, :MEMBERS] = noise_ref[k]
        noise_wide[:, MEMBERS:] = noise_ref[k]
        rhs = col(k, 4) + jnp.sqrt(var) * noise_wide[...] - prior
        both = inverse_var * jnp.where(low_lanes, anom, rhs)
        aug = scale * dot_n(anom.T[:MEMBERS], both, HIGHEST)
        aug += jnp.where(iota(aug.shape, 0) == iota(aug.shape, 1), 1.0, 0.0)
        solved = gauss_jordan(aug)
        solved = jnp.where(
            iota(solved.shape, 1) < MEMBERS, pltpu.roll(solved, MEMBERS, 1), solved
        )
        white = inverse_var * (rhs - dot_n(anom[:, :MEMBERS], solved, HIGHEST))

        for later in range(k + 1, BATCH_GROUPS):
            cov = dot_t(priors[later][:, :MEMBERS], anom[:, :MEMBERS], HIGHEST)
            cov = cov * rho_of(col(later, 0), col(later, 1), k)
            priors[later] = priors[later] + dot_n(cov, white, HIGHEST)

        wide_anom = jnp.concatenate(
            [jnp.where(low_lanes, anom, 0.0), jnp.where(low_lanes, 0.0, anom)], axis=0
        )
        wide_white = jnp.concatenate(
            [jnp.where(low_lanes, white, 0.0), jnp.where(low_lanes, 0.0, white)], axis=0
        )
        rho = []
        for i in range(tile_lat):
            lat_at = (ilat * tile_lat + i).astype(jnp.float32)
            lon_at = (ilon * tile_lon + iota((tile_lon, 1), 0)).astype(jnp.float32)
            one = rho_of(lat_at, lon_at, k)
            rho.append(jnp.concatenate([one, one], axis=1)[None])
        rho = jnp.stack(rho, axis=0)

        x = state_ref[...] if k == 0 else x_ref[...]
        x_high, x_low = split(x)
        a_high, a_low = split(wide_anom)
        cov = dot_t(
            jnp.concatenate([x_high, x_low], axis=1), jnp.concatenate([a_high, a_high], axis=1)
        ) + dot_t(x_high, a_low)
        cov = cov.reshape(tile_lat, pairs, tile_lon, 2 * count) * rho
        cov = cov.reshape(tile_lat * pairs * tile_lon, 2 * count)
        c_high, c_low = split(cov)
        w_high, w_low = split(wide_white)
        two = dot_n(c_high, jnp.concatenate([w_high, w_low], axis=1))
        new = x + (two[:, :LANES] + two[:, LANES:] + dot_n(c_low, w_high))
        if k + 1 < BATCH_GROUPS:
            x_ref[...] = new
        else:
            for i in range(tile_lat):
                for p in range(pairs):
                    at = (i * pairs + p) * tile_lon
                    out_ref[i, :, p * LANES : (p + 1) * LANES] = new[at : at + tile_lon]


def body(
    ensemble,
    northward_wind,
    eastward_wind,
    spreading_strength,
    measurement_home_subdomain,
    obs_site,
    obs_class,
    cutoff_table,
    obs_value,
    obs_var,
    obs_noise,
):
    lat_n = lax.axis_size("lat")
    lon_n = lax.axis_size("lon")
    tile_lat, tile_lon, width = ensemble.shape
    rows = tile_lat * tile_lon * width // LANES
    count = obs_site.shape[1]
    vmem = pl.BlockSpec(memory_space=pltpu.VMEM)
    smem = pl.BlockSpec(memory_space=pltpu.SMEM)
    f32 = jnp.float32
    dma = pltpu.SemaphoreType.DMA
    state, gathered, rank = pl.pallas_call(
        functools.partial(forecast_kernel, lat_n, lon_n),
        out_shape=(
            jax.ShapeDtypeStruct((rows, LANES), f32),
            jax.ShapeDtypeStruct((lat_n * lon_n * SLOT_ROWS, LANES), f32),
            jax.ShapeDtypeStruct((8, count), f32),
        ),
        in_specs=[vmem] * 6,
        out_specs=(vmem, vmem, vmem),
        scratch_shapes=[
            pltpu.VMEM((SECTIONS - 1, tile_lat, tile_lon, width), f32),
            pltpu.VMEM((SECTIONS, 2, tile_lat, width), f32),
            pltpu.VMEM((SECTIONS, 2, tile_lon, width), f32),
            pltpu.VMEM((SECTIONS, 2, tile_lat, width), f32),
            pltpu.VMEM((lat_n, lon_n, SLOT_ROWS, LANES), f32),
            dma((SECTIONS, 4)),
            dma((SECTIONS, 4)),
            dma((lon_n - 1,)),
            dma((lon_n - 1,)),
            dma((lat_n - 1,)),
            dma((lat_n - 1,)),
        ],
        compiler_params=pltpu.CompilerParams(
            collective_id=0, has_side_effects=True, vmem_limit_bytes=32 << 20
        ),
    )(
        ensemble,
        northward_wind,
        eastward_wind,
        spreading_strength,
        measurement_home_subdomain,
        obs_site,
    )
    return pl.pallas_call(
        functools.partial(update_kernel, lat_n, lon_n),
        out_shape=jax.ShapeDtypeStruct(ensemble.shape, f32),
        in_specs=[vmem] * 6 + [smem] + [vmem] * 3,
        out_specs=vmem,
        scratch_shapes=[pltpu.VMEM((rows, LANES), f32), pltpu.VMEM((count, LANES), f32)],
        compiler_params=pltpu.CompilerParams(vmem_limit_bytes=48 << 20),
    )(
        state,
        gathered,
        rank,
        measurement_home_subdomain,
        obs_site,
        obs_class,
        cutoff_table,
        obs_value,
        obs_var,
        obs_noise,
    )


def solution(mesh):
    placed = (
        P("lat", "lon", None),
        P("lat", "lon"),
        P("lat", "lon"),
        P("lat", "lon"),
        P(),
        P(),
        P(),
        P(),
        P(),
        P(),
        P(),
    )
    return jax.shard_map(
        body, mesh=mesh, in_specs=placed, out_specs=P("lat", "lon", None), check_vma=False
    )
```

```python
import functools

import jax
import jax.numpy as jnp
from jax import lax
from jax.experimental import pallas as pl
from jax.experimental.pallas import tpu as pltpu
from jax.sharding import PartitionSpec as P

LEV = 28
MEMBERS = 64
SECTIONS = 2
BATCH_GROUPS = 3
CAP = 4
LANES = 128
PIVOTS = 4

advect_coef = 0.2
MESH = pl.DeviceIdType.MESH
SLOT_ROWS = -(-(BATCH_GROUPS * CAP) // 16) * 8


def floor_div(value, divisor):
    return jnp.floor((value + 0.5) * (1.0 / divisor))


def dot_t(a, b):
    return lax.dot_general(
        a, b, (((1,), (1,)), ((), ())), preferred_element_type=jnp.float32
    )


def dot_n(a, b):
    return lax.dot_general(
        a, b, (((1,), (0,)), ((), ())), preferred_element_type=jnp.float32
    )


def split(value):
    high = value.astype(jnp.bfloat16)
    low = (value - high.astype(jnp.float32)).astype(jnp.bfloat16)
    return high, low


def dot3(dot, a, b):
    a_high, a_low = split(a)
    b_high, b_low = split(b)
    return dot(a_high, b_high) + (dot(a_high, b_low) + dot(a_low, b_high))


def pick_rows(chosen, table):
    high, low = split(table)
    both = dot_n(chosen, jnp.concatenate([high, low], axis=1))
    return both[:, : table.shape[1]] + both[:, table.shape[1] :]


def iota(shape, dim):
    return lax.broadcasted_iota(jnp.int32, shape, dim)


def column(row):
    n = row.shape[1]
    return jnp.sum(
        jnp.where(iota((n, n), 0) == iota((n, n), 1), row, 0.0), axis=1, keepdims=True
    )


def forecast_kernel(
    lat_n,
    lon_n,
    ens_hbm,
    north_hbm,
    east_hbm,
    spread_hbm,
    owner_hbm,
    site_hbm,
    class_hbm,
    value_hbm,
    var_hbm,
    cutoff_hbm,
    state_ref,
    gather_ref,
    meta_ref,
    ens_ref,
    north_ref,
    east_ref,
    spread_ref,
    owner_ref,
    site_ref,
    class_ref,
    value_ref,
    var_ref,
    cutoff_ref,
    load_sem,
    mid,
    edge,
    halo_lat,
    halo_lon,
    slots,
    send_sem,
    recv_sem,
    lon_send,
    lon_recv,
    lat_send,
    lat_recv,
):
    ilat = lax.axis_index("lat")
    ilon = lax.axis_index("lon")
    tile_lat, tile_lon, width = ens_ref.shape
    pairs = width // LANES
    lon_peers = [lax.rem(ilon + d, lon_n) for d in range(1, lon_n)]
    lat_peers = [lax.rem(ilat + d, lat_n) for d in range(1, lat_n)]

    barrier = pltpu.get_barrier_semaphore()
    for peer in lon_peers:
        pl.semaphore_signal(barrier, inc=1, device_id=(ilat, peer), device_id_type=MESH)
    for peer in lat_peers:
        pl.semaphore_signal(barrier, inc=1, device_id=(peer, ilon), device_id_type=MESH)

    loads = []
    for n, (a, b) in enumerate(
        (
            (ens_hbm, ens_ref),
            (spread_hbm, spread_ref),
            (north_hbm, north_ref),
            (east_hbm, east_ref),
            (owner_hbm, owner_ref),
            (site_hbm, site_ref),
            (class_hbm, class_ref),
            (cutoff_hbm, cutoff_ref),
            (value_hbm, value_ref),
            (var_hbm, var_ref),
        )
    ):
        load = pltpu.make_async_copy(a, b, load_sem.at[n])
        load.start()
        loads.append(load)

    def fill_edges(section, src):
        for i in range(tile_lat):
            edge[section, 0, i : i + 1, :] = src[i, tile_lon - 1 : tile_lon, :]
            edge[section, 1, i : i + 1, :] = src[i, 0:1, :]

    up = lax.rem(ilat + 1, lat_n)
    down = lax.rem(ilat + lat_n - 1, lat_n)
    right = lax.rem(ilon + 1, lon_n)
    left = lax.rem(ilon + lon_n - 1, lon_n)

    def send(section, n, a, b, device):
        copy = pltpu.make_async_remote_copy(
            src_ref=a,
            dst_ref=b,
            send_sem=send_sem.at[section, n],
            recv_sem=recv_sem.at[section, n],
            device_id=device,
            device_id_type=MESH,
        )
        copy.start()
        return copy

    def send_rows(section, src):
        return [
            send(section, 0, src.at[tile_lat - 1], halo_lat.at[section, 0], (up, ilon)),
            send(section, 1, src.at[0], halo_lat.at[section, 1], (down, ilon)),
        ]

    def send_columns(section):
        return [
            send(section, 2, edge.at[section, 0], halo_lon.at[section, 0], (ilat, right)),
            send(section, 3, edge.at[section, 1], halo_lon.at[section, 1], (ilat, left)),
        ]

    pl.semaphore_wait(barrier, len(lon_peers) + len(lat_peers))
    copies = send_rows(0, ens_hbm)
    loads[0].wait()
    fill_edges(0, ens_ref)
    copies += send_columns(0)
    for load in loads[1:]:
        load.wait()

    same = iota((tile_lon, tile_lon), 0) == iota((tile_lon, tile_lon), 1)
    coef = []
    for i in range(tile_lat):
        s, n, e = (
            jnp.sum(jnp.where(same, ref[i : i + 1, :], 0.0), axis=1, keepdims=True)
            for ref in (spread_ref, north_ref, east_ref)
        )
        n = advect_coef * n
        e = advect_coef * e
        coef.append((1.0 - 4.0 * s, s - n, s + n, s - e, s + e))

    count = owner_ref.shape[1]
    me = (ilat * lon_n + ilon).astype(jnp.float32)
    half = SLOT_ROWS
    slot_iota = iota((2 * half, count), 0)
    slot_id = (2 * (slot_iota % half) + slot_iota // half).astype(jnp.float32)
    slot_row = jnp.zeros((2 * half, 1), jnp.float32)
    slot_odd = jnp.zeros((2 * half, 1), jnp.float32)
    for k in range(BATCH_GROUPS):
        owner = owner_ref[k : k + 1, :].astype(jnp.float32)
        site = site_ref[k : k + 1, :].astype(jnp.float32)
        before = iota((count, count), 0) < iota((count, count), 1)
        earlier = (column(owner) == owner) & before
        rank = jnp.sum(jnp.where(earlier, 1.0, 0.0), axis=0, keepdims=True)
        cell = floor_div(site, LEV)
        level = site - LEV * cell
        cell_lat = floor_div(cell, tile_lon)
        cell_lon = cell - tile_lon * cell_lat
        pair = floor_div(level, 2)
        row = (cell_lat * pairs + pair) * tile_lon + cell_lon
        mine = (owner == me) & (slot_id == rank + float(CAP * k))
        slot_row += jnp.sum(jnp.where(mine, row, 0.0), axis=1, keepdims=True)
        slot_odd += jnp.sum(jnp.where(mine, level - 2.0 * pair, 0.0), axis=1, keepdims=True)
        tile_row = floor_div(owner, lon_n)
        radius = jnp.zeros((1, count), jnp.float32)
        for c in range(cutoff_ref.shape[0]):
            radius = jnp.where(
                class_ref[k : k + 1, :] == c, cutoff_ref[c].astype(jnp.float32), radius
            )
        slot = rank + float(CAP * k)
        slot_half = floor_div(slot, 2)
        meta = (
            tile_row * tile_lat + cell_lat,
            (owner - lon_n * tile_row) * tile_lon + cell_lon,
            owner * SLOT_ROWS + slot_half,
            slot - 2.0 * slot_half,
            value_ref[k : k + 1, :],
            var_ref[k : k + 1, :],
            1.0 / radius,
            jnp.zeros((1, count), jnp.float32),
        )
        meta_ref[8 * k : 8 * k + 8, :] = jnp.concatenate(meta, axis=0)
    rows = tile_lat * width // LANES * tile_lon
    pick = jnp.where(
        iota((2 * half, rows), 1).astype(jnp.float32) == slot_row, 1.0, 0.0
    ).astype(jnp.bfloat16)

    src = ens_ref
    for section in range(SECTIONS):
        for copy in copies:
            copy.wait()
        last = section == SECTIONS - 1
        for i in range(tile_lat):
            centre, c_n, c_s, c_e, c_w = coef[i]
            here = src[i]
            if i + 1 < tile_lat:
                above = src[i + 1]
            else:
                above = jnp.where(ilat == lat_n - 1, 0.0, halo_lat[section, 1])
            if i > 0:
                below = src[i - 1]
            else:
                below = jnp.where(ilat == 0, 0.0, halo_lat[section, 0])
            east = jnp.concatenate([here[1:], halo_lon[section, 1, i : i + 1, :]], axis=0)
            west = jnp.concatenate([halo_lon[section, 0, i : i + 1, :], here[:-1]], axis=0)
            new = centre * here + c_n * above + c_s * below + c_e * east + c_w * west
            if last:
                for p in range(pairs):
                    at = (i * pairs + p) * tile_lon
                    state_ref[at : at + tile_lon, :] = new[:, p * LANES : (p + 1) * LANES]
            else:
                mid[section, i] = new
        if not last:
            src = mid.at[section]
            copies = send_rows(section + 1, src)
            fill_edges(section + 1, src)
            copies += send_columns(section + 1)

    taken = pick_rows(pick, state_ref[...])
    first, second = taken[:half], taken[half:]
    first = jnp.where(slot_odd[:half] < 0.5, first, pltpu.roll(first, MEMBERS, 1))
    second = jnp.where(slot_odd[half:] > 0.5, second, pltpu.roll(second, MEMBERS, 1))
    low_half = iota((half, LANES), 1) < MEMBERS
    slots[ilat, ilon] = jnp.where(low_half, first, second)

    def share(src_at, peers, sends, recvs, device_of):
        out = []
        for n, peer in enumerate(peers):
            copy = pltpu.make_async_remote_copy(
                src_ref=src_at,
                dst_ref=src_at,
                send_sem=sends.at[n],
                recv_sem=recvs.at[n],
                device_id=device_of(peer),
                device_id_type=MESH,
            )
            copy.start()
            out.append(copy)
        for copy in out:
            copy.wait()

    share(slots.at[ilat, ilon], lon_peers, lon_send, lon_recv, lambda peer: (ilat, peer))
    share(slots.at[ilat], lat_peers, lat_send, lat_recv, lambda peer: (peer, ilon))
    gather_ref[...] = slots[...].reshape(gather_ref.shape)


def taper(dist, inverse_radius):
    z = dist * inverse_radius
    inner = 1.0 + z * z * (-5.0 / 3.0 + z * (0.625 + z * (0.5 - 0.25 * z)))
    o = jnp.maximum(z, 1.0)
    outer = (
        4.0
        + o * (-5.0 + o * (5.0 / 3.0 + o * (0.625 + o * (-0.5 + o * (1.0 / 12.0)))))
        - (2.0 / 3.0) / o
    )
    return jnp.where(z <= 1.0, inner, jnp.where(z < 2.0, outer, 0.0))


def gauss_jordan(aug):
    size = aug.shape[0]
    blocks = [aug[i : i + 8] for i in range(0, size, 8)]
    sub = iota((8, LANES), 0)
    for base in range(0, size, PIVOTS):
        home, at = base // 8, base % 8
        cols = [
            [jnp.broadcast_to(block[:, base + j : base + j + 1], (8, LANES)) for block in blocks]
            for j in range(PIVOTS)
        ]
        rows = [blocks[home][at + i : at + i + 1] for i in range(PIVOTS)]
        c = [[cols[j][home][at + i : at + i + 1] for j in range(PIVOTS)] for i in range(PIVOTS)]
        for i in range(PIVOTS):
            inverse = 1.0 / c[i][i]
            rows[i] = rows[i] * inverse
            for j in range(i + 1, PIVOTS):
                c[i][j] = c[i][j] * inverse
            for r in range(PIVOTS):
                if r != i:
                    f = c[r][i]
                    rows[r] = rows[r] - f * rows[i]
                    for j in range(i + 1, PIVOTS):
                        c[r][j] = c[r][j] - f * c[i][j]
        wide = [jnp.broadcast_to(row, (8, LANES)) for row in rows]
        for b in range(len(blocks)):
            new = blocks[b]
            for j in range(PIVOTS):
                new = new - cols[j][b] * wide[j]
            if b == home:
                for j in range(PIVOTS):
                    new = jnp.where(sub == at + j, wide[j], new)
            blocks[b] = new
    return jnp.concatenate(blocks, axis=0)


def update_kernel(
    lat_n,
    lon_n,
    state_ref,
    gather_ref,
    meta_ref,
    noise_ref,
    out_ref,
    x_ref,
):
    tile_lat, tile_lon, width = out_ref.shape
    pairs = width // LANES
    ilat = lax.axis_index("lat")
    ilon = lax.axis_index("lon")
    lon_cells = float(tile_lon * lon_n)
    count = meta_ref.shape[1]
    scale = 1.0 / (MEMBERS - 1)
    low_lanes = iota((count, LANES), 1) < MEMBERS

    table = meta_ref[...].T
    rows_of = [
        [meta_ref[8 * k + n : 8 * k + n + 1, :] for n in (0, 1, 6)] for k in range(BATCH_GROUPS)
    ]

    def col(k, n):
        return table[:, 8 * k + n : 8 * k + n + 1]

    def rho_of(lat_at, lon_at, k):
        glat, glon, inverse_radius = rows_of[k]
        dlat = jnp.abs(lat_at - glat)
        dlon = jnp.abs(lon_at - glon)
        dlon = jnp.minimum(dlon, lon_cells - dlon)
        return scale * taper(jnp.sqrt(dlat * dlat + dlon * dlon), inverse_radius)

    slots = gather_ref.shape[0]
    priors = []
    for k in range(BATCH_GROUPS):
        pick = jnp.where(iota((count, slots), 1).astype(jnp.float32) == col(k, 2), 1.0, 0.0)
        taken = pick_rows(pick.astype(jnp.bfloat16), gather_ref[...])
        turned = pltpu.roll(taken, MEMBERS, 1)
        odd = col(k, 3) > 0.5
        priors.append(jnp.where(odd != low_lanes, taken, turned))

    for k in range(BATCH_GROUPS):
        prior = priors[k]
        var = col(k, 5)
        inverse_var = 1.0 / var
        anom = prior - jnp.mean(prior, axis=1, keepdims=True)
        noise = jnp.concatenate([noise_ref[k], noise_ref[k]], axis=0).T
        rhs = col(k, 4) + jnp.sqrt(var) * noise - prior
        both = inverse_var * jnp.where(low_lanes, anom, rhs)
        aug = scale * dot3(dot_n, anom.T[:MEMBERS], both)
        aug += jnp.where(iota(aug.shape, 0) == iota(aug.shape, 1), 1.0, 0.0)
        solved = gauss_jordan(aug)
        solved = jnp.where(
            iota(solved.shape, 1) < MEMBERS, pltpu.roll(solved, MEMBERS, 1), solved
        )
        white = inverse_var * (rhs - dot3(dot_n, anom[:, :MEMBERS], solved))

        for later in range(k + 1, BATCH_GROUPS):
            cov = dot3(dot_t, priors[later][:, :MEMBERS], anom[:, :MEMBERS])
            cov = cov * rho_of(col(later, 0), col(later, 1), k)
            priors[later] = priors[later] + dot3(dot_n, cov, white)

        wide_anom = jnp.concatenate(
            [jnp.where(low_lanes, anom, 0.0), jnp.where(low_lanes, 0.0, anom)], axis=0
        )
        wide_white = jnp.concatenate(
            [jnp.where(low_lanes, white, 0.0), jnp.where(low_lanes, 0.0, white)], axis=0
        )
        rho = []
        for i in range(tile_lat):
            lat_at = (ilat * tile_lat + i).astype(jnp.float32)
            lon_at = (ilon * tile_lon + iota((tile_lon, 1), 0)).astype(jnp.float32)
            one = rho_of(lat_at, lon_at, k)
            rho.append(jnp.concatenate([one, one], axis=1)[None])
        rho = jnp.stack(rho, axis=0)

        x = state_ref[...] if k == 0 else x_ref[...]
        x_high, x_low = split(x)
        a_high, a_low = split(wide_anom)
        cov = dot_t(
            jnp.concatenate([x_high, x_low], axis=1), jnp.concatenate([a_high, a_high], axis=1)
        ) + dot_t(x_high, a_low)
        cov = cov.reshape(tile_lat, pairs, tile_lon, 2 * count) * rho
        cov = cov.reshape(tile_lat * pairs * tile_lon, 2 * count)
        c_high, c_low = split(cov)
        w_high, w_low = split(wide_white)
        two = dot_n(c_high, jnp.concatenate([w_high, w_low], axis=1))
        new = x + (two[:, :LANES] + two[:, LANES:] + dot_n(c_low, w_high))
        if k + 1 < BATCH_GROUPS:
            x_ref[...] = new
        else:
            for i in range(tile_lat):
                for p in range(pairs):
                    at = (i * pairs + p) * tile_lon
                    out_ref[i, :, p * LANES : (p + 1) * LANES] = new[at : at + tile_lon]


def body(
    ensemble,
    northward_wind,
    eastward_wind,
    spreading_strength,
    measurement_home_subdomain,
    obs_site,
    obs_class,
    cutoff_table,
    obs_value,
    obs_var,
    obs_noise,
):
    lat_n = lax.axis_size("lat")
    lon_n = lax.axis_size("lon")
    tile_lat, tile_lon, width = ensemble.shape
    rows = tile_lat * tile_lon * width // LANES
    count = obs_site.shape[1]
    vmem = pl.BlockSpec(memory_space=pltpu.VMEM)
    f32 = jnp.float32
    dma = pltpu.SemaphoreType.DMA
    loaded = (
        ensemble,
        northward_wind,
        eastward_wind,
        spreading_strength,
        measurement_home_subdomain,
        obs_site,
        obs_class,
        obs_value,
        obs_var,
        cutoff_table,
    )
    state, gathered, meta = pl.pallas_call(
        functools.partial(forecast_kernel, lat_n, lon_n),
        out_shape=(
            jax.ShapeDtypeStruct((rows, LANES), f32),
            jax.ShapeDtypeStruct((lat_n * lon_n * SLOT_ROWS, LANES), f32),
            jax.ShapeDtypeStruct((8 * BATCH_GROUPS, count), f32),
        ),
        in_specs=[pl.BlockSpec(memory_space=pltpu.HBM)] * len(loaded),
        out_specs=(vmem, vmem, vmem),
        scratch_shapes=[pltpu.VMEM(a.shape, a.dtype) for a in loaded[:-1]]
        + [
            pltpu.SMEM(cutoff_table.shape, cutoff_table.dtype),
            dma((len(loaded),)),
            pltpu.VMEM((SECTIONS - 1, tile_lat, tile_lon, width), f32),
            pltpu.VMEM((SECTIONS, 2, tile_lat, width), f32),
            pltpu.VMEM((SECTIONS, 2, tile_lon, width), f32),
            pltpu.VMEM((SECTIONS, 2, tile_lat, width), f32),
            pltpu.VMEM((lat_n, lon_n, SLOT_ROWS, LANES), f32),
            dma((SECTIONS, 4)),
            dma((SECTIONS, 4)),
            dma((lon_n - 1,)),
            dma((lon_n - 1,)),
            dma((lat_n - 1,)),
            dma((lat_n - 1,)),
        ],
        compiler_params=pltpu.CompilerParams(
            collective_id=0, has_side_effects=True, vmem_limit_bytes=32 << 20
        ),
    )(*loaded)
    return pl.pallas_call(
        functools.partial(update_kernel, lat_n, lon_n),
        out_shape=jax.ShapeDtypeStruct(ensemble.shape, f32),
        in_specs=[vmem] * 4,
        out_specs=vmem,
        scratch_shapes=[pltpu.VMEM((rows, LANES), f32)],
        compiler_params=pltpu.CompilerParams(vmem_limit_bytes=48 << 20),
    )(state, gathered, meta, jnp.swapaxes(obs_noise, 1, 2))


def solution(mesh):
    placed = (
        P("lat", "lon", None),
        P("lat", "lon"),
        P("lat", "lon"),
        P("lat", "lon"),
        P(),
        P(),
        P(),
        P(),
        P(),
        P(),
        P(),
    )
    return jax.shard_map(
        body, mesh=mesh, in_specs=placed, out_specs=P("lat", "lon", None), check_vma=False
    )
```

```python
import functools

import jax
import jax.numpy as jnp
from jax import lax
from jax.experimental import pallas as pl
from jax.experimental.pallas import tpu as pltpu
from jax.sharding import PartitionSpec as P

LEV = 28
MEMBERS = 64
BATCH_GROUPS = 3
CAP = 4
LANES = 128
PIVOTS = 4

advect_coef = 0.2
MESH = pl.DeviceIdType.MESH
SLOT_ROWS = -(-(BATCH_GROUPS * CAP) // 16) * 8


def floor_div(value, divisor):
    return jnp.floor((value + 0.5) * (1.0 / divisor))


def dot_t(a, b):
    return lax.dot_general(
        a, b, (((1,), (1,)), ((), ())), preferred_element_type=jnp.float32
    )


def dot_n(a, b):
    return lax.dot_general(
        a, b, (((1,), (0,)), ((), ())), preferred_element_type=jnp.float32
    )


def split(value):
    high = value.astype(jnp.bfloat16)
    low = (value - high.astype(jnp.float32)).astype(jnp.bfloat16)
    return high, low


def dot3(dot, a, b):
    a_high, a_low = split(a)
    b_high, b_low = split(b)
    return dot(a_high, b_high) + (dot(a_high, b_low) + dot(a_low, b_high))


def pick_rows(chosen, table):
    high, low = split(table)
    both = dot_n(chosen, jnp.concatenate([high, low], axis=1))
    return both[:, : table.shape[1]] + both[:, table.shape[1] :]


def iota(shape, dim):
    return lax.broadcasted_iota(jnp.int32, shape, dim)


def column(row):
    n = row.shape[1]
    return jnp.sum(
        jnp.where(iota((n, n), 0) == iota((n, n), 1), row, 0.0), axis=1, keepdims=True
    )


def forecast_kernel(
    lat_n,
    lon_n,
    ens_ref,
    spread_ref,
    north_ref,
    east_ref,
    owner_ref,
    site_ref,
    class_ref,
    value_ref,
    var_ref,
    cutoff_ref,
    state_ref,
    gather_ref,
    meta_ref,
    edge,
    corner,
    wind,
    halo_lat,
    halo_lon,
    halo_corner,
    halo_wind,
    slots,
    send_sem,
    recv_sem,
    lon_send,
    lon_recv,
    lat_send,
    lat_recv,
):
    ilat = lax.axis_index("lat")
    ilon = lax.axis_index("lon")
    tile_lat, tile_lon, width = ens_ref.shape
    pairs = width // LANES
    lon_peers = [lax.rem(ilon + d, lon_n) for d in range(1, lon_n)]
    lat_peers = [lax.rem(ilat + d, lat_n) for d in range(1, lat_n)]

    up = lax.rem(ilat + 1, lat_n)
    down = lax.rem(ilat + lat_n - 1, lat_n)
    right = lax.rem(ilon + 1, lon_n)
    left = lax.rem(ilon + lon_n - 1, lon_n)
    diagonal = [(up, right), (up, left), (down, right), (down, left)]

    barrier = pltpu.get_barrier_semaphore()
    for peer in lon_peers:
        pl.semaphore_signal(barrier, inc=1, device_id=(ilat, peer), device_id_type=MESH)
    for peer in lat_peers:
        pl.semaphore_signal(barrier, inc=1, device_id=(peer, ilon), device_id_type=MESH)

    for device in diagonal:
        pl.semaphore_signal(barrier, inc=1, device_id=device, device_id_type=MESH)

    top, end = tile_lat - 1, tile_lon - 1
    for i in range(tile_lat):
        for c in range(2):
            at = c * tile_lat + i
            edge[0, at : at + 1, :] = ens_ref[i, end - 1 + c : end + c, :]
            edge[1, at : at + 1, :] = ens_ref[i, c : c + 1, :]
    for n, (i, j) in enumerate(((top, end), (top, 0), (0, end), (0, 0))):
        corner[n] = ens_ref[i, j : j + 1, :]
    for n, ref in enumerate((spread_ref, north_ref, east_ref)):
        wind[n] = ref[...]

    pl.semaphore_wait(barrier, len(lon_peers) + len(lat_peers) + len(diagonal))
    moves = [
        (ens_ref.at[pl.ds(tile_lat - 2, 2)], halo_lat.at[0], (up, ilon)),
        (ens_ref.at[pl.ds(0, 2)], halo_lat.at[1], (down, ilon)),
        (edge.at[0], halo_lon.at[0], (ilat, right)),
        (edge.at[1], halo_lon.at[1], (ilat, left)),
        (wind, halo_wind.at[0], (up, ilon)),
        (wind, halo_wind.at[1], (down, ilon)),
        (wind, halo_wind.at[2], (ilat, right)),
        (wind, halo_wind.at[3], (ilat, left)),
    ] + [(corner.at[n], halo_corner.at[n], device) for n, device in enumerate(diagonal)]
    copies = []
    for n, (a, b, device) in enumerate(moves):
        copy = pltpu.make_async_remote_copy(
            src_ref=a,
            dst_ref=b,
            send_sem=send_sem.at[n],
            recv_sem=recv_sem.at[n],
            device_id=device,
            device_id_type=MESH,
        )
        copy.start()
        copies.append(copy)

    same = iota((tile_lon, tile_lon), 0) == iota((tile_lon, tile_lon), 1)

    def weights(s, n, e):
        n = advect_coef * n
        e = advect_coef * e
        return (1.0 - 4.0 * s, s - n, s + n, s - e, s + e)

    def row_weights(rows):
        return weights(
            *(jnp.sum(jnp.where(same, row, 0.0), axis=1, keepdims=True) for row in rows)
        )

    coef = [
        row_weights([ref[i : i + 1, :] for ref in (spread_ref, north_ref, east_ref)])
        for i in range(tile_lat)
    ]

    count = owner_ref.shape[1]
    me = (ilat * lon_n + ilon).astype(jnp.float32)
    half = SLOT_ROWS
    slot_iota = iota((2 * half, count), 0)
    slot_id = (2 * (slot_iota % half) + slot_iota // half).astype(jnp.float32)
    slot_row = jnp.zeros((2 * half, 1), jnp.float32)
    slot_odd = jnp.zeros((2 * half, 1), jnp.float32)
    for k in range(BATCH_GROUPS):
        owner = owner_ref[k : k + 1, :].astype(jnp.float32)
        site = site_ref[k : k + 1, :].astype(jnp.float32)
        before = iota((count, count), 0) < iota((count, count), 1)
        earlier = (column(owner) == owner) & before
        rank = jnp.sum(jnp.where(earlier, 1.0, 0.0), axis=0, keepdims=True)
        cell = floor_div(site, LEV)
        level = site - LEV * cell
        cell_lat = floor_div(cell, tile_lon)
        cell_lon = cell - tile_lon * cell_lat
        pair = floor_div(level, 2)
        row = (cell_lat * pairs + pair) * tile_lon + cell_lon
        mine = (owner == me) & (slot_id == rank + float(CAP * k))
        slot_row += jnp.sum(jnp.where(mine, row, 0.0), axis=1, keepdims=True)
        slot_odd += jnp.sum(jnp.where(mine, level - 2.0 * pair, 0.0), axis=1, keepdims=True)
        tile_row = floor_div(owner, lon_n)
        radius = jnp.zeros((1, count), jnp.float32)
        for c in range(cutoff_ref.shape[0]):
            radius = jnp.where(
                class_ref[k : k + 1, :] == c, cutoff_ref[c].astype(jnp.float32), radius
            )
        slot = rank + float(CAP * k)
        slot_half = floor_div(slot, 2)
        meta = (
            tile_row * tile_lat + cell_lat,
            (owner - lon_n * tile_row) * tile_lon + cell_lon,
            owner * SLOT_ROWS + slot_half,
            slot - 2.0 * slot_half,
            value_ref[k : k + 1, :],
            var_ref[k : k + 1, :],
            1.0 / radius,
            jnp.zeros((1, count), jnp.float32),
        )
        meta_ref[8 * k : 8 * k + 8, :] = jnp.concatenate(meta, axis=0)
    rows = tile_lat * width // LANES * tile_lon
    pick = jnp.where(
        iota((2 * half, rows), 1).astype(jnp.float32) == slot_row, 1.0, 0.0
    ).astype(jnp.bfloat16)

    for copy in copies:
        copy.wait()

    def advance(weight, here, above, below, east, west):
        centre, c_n, c_s, c_e, c_w = weight
        return centre * here + c_n * above + c_s * below + c_e * east + c_w * west

    def along_row(weight, here, above, below, east_end, west_end):
        east = jnp.concatenate([here[1:], east_end], axis=0)
        west = jnp.concatenate([west_end, here[:-1]], axis=0)
        return advance(weight, here, above, below, east, west)

    first_tile, last_tile = ilat == 0, ilat == lat_n - 1
    below_1, below_2 = (jnp.where(first_tile, 0.0, halo_lat[0, n]) for n in (1, 0))
    above_1, above_2 = (jnp.where(last_tile, 0.0, halo_lat[1, n]) for n in (0, 1))
    corner_bw, corner_be = (jnp.where(first_tile, 0.0, halo_corner[n]) for n in (0, 1))
    corner_aw, corner_ae = (jnp.where(last_tile, 0.0, halo_corner[n]) for n in (2, 3))
    west_2, west_1 = halo_lon[0, :tile_lat], halo_lon[0, tile_lat:]
    east_1, east_2 = halo_lon[1, :tile_lat], halo_lon[1, tile_lat:]
    own_east, own_west = edge[0, tile_lat:], edge[1, :tile_lat]

    rows = [below_1] + [ens_ref[i] for i in range(tile_lat)] + [above_1]
    mid = [
        along_row(
            coef[i], rows[i + 1], rows[i + 2], rows[i], east_1[i : i + 1], west_1[i : i + 1]
        )
        for i in range(tile_lat)
    ]
    weight = row_weights([halo_wind[0, n, top : top + 1, :] for n in range(3)])
    mid_below = along_row(weight, below_1, rows[1], below_2, corner_be, corner_bw)
    weight = row_weights([halo_wind[1, n, 0:1, :] for n in range(3)])
    mid_above = along_row(weight, above_1, above_2, rows[tile_lat], corner_ae, corner_aw)
    mid_below = jnp.where(first_tile, 0.0, mid_below)
    mid_above = jnp.where(last_tile, 0.0, mid_above)

    def along_column(weight, here, above_end, below_end, east, west):
        above = jnp.concatenate([here[1:], above_end], axis=0)
        below = jnp.concatenate([below_end, here[:-1]], axis=0)
        return advance(weight, here, above, below, east, west)

    weight = weights(*(halo_wind[2, n, :, end : end + 1] for n in range(3)))
    mid_west = along_column(weight, west_1, corner_aw, corner_bw, own_west, west_2)
    weight = weights(*(halo_wind[3, n, :, 0:1] for n in range(3)))
    mid_east = along_column(weight, east_1, corner_ae, corner_be, east_2, own_east)

    rows = [mid_below] + mid + [mid_above]
    for i in range(tile_lat):
        new = along_row(
            coef[i], rows[i + 1], rows[i + 2], rows[i], mid_east[i : i + 1], mid_west[i : i + 1]
        )
        for p in range(pairs):
            at = (i * pairs + p) * tile_lon
            state_ref[at : at + tile_lon, :] = new[:, p * LANES : (p + 1) * LANES]

    taken = pick_rows(pick, state_ref[...])
    first, second = taken[:half], taken[half:]
    first = jnp.where(slot_odd[:half] < 0.5, first, pltpu.roll(first, MEMBERS, 1))
    second = jnp.where(slot_odd[half:] > 0.5, second, pltpu.roll(second, MEMBERS, 1))
    low_half = iota((half, LANES), 1) < MEMBERS
    slots[ilat, ilon] = jnp.where(low_half, first, second)

    def share(src_at, peers, sends, recvs, device_of):
        out = []
        for n, peer in enumerate(peers):
            copy = pltpu.make_async_remote_copy(
                src_ref=src_at,
                dst_ref=src_at,
                send_sem=sends.at[n],
                recv_sem=recvs.at[n],
                device_id=device_of(peer),
                device_id_type=MESH,
            )
            copy.start()
            out.append(copy)
        for copy in out:
            copy.wait()

    share(slots.at[ilat, ilon], lon_peers, lon_send, lon_recv, lambda peer: (ilat, peer))
    share(slots.at[ilat], lat_peers, lat_send, lat_recv, lambda peer: (peer, ilon))
    gather_ref[...] = slots[...].reshape(gather_ref.shape)


def taper(dist, inverse_radius):
    z = dist * inverse_radius
    inner = 1.0 + z * z * (-5.0 / 3.0 + z * (0.625 + z * (0.5 - 0.25 * z)))
    o = jnp.maximum(z, 1.0)
    outer = (
        4.0
        + o * (-5.0 + o * (5.0 / 3.0 + o * (0.625 + o * (-0.5 + o * (1.0 / 12.0)))))
        - (2.0 / 3.0) / o
    )
    return jnp.where(z <= 1.0, inner, jnp.where(z < 2.0, outer, 0.0))


def gauss_jordan(aug):
    size = aug.shape[0]
    blocks = [aug[i : i + 8] for i in range(0, size, 8)]
    sub = iota((8, LANES), 0)
    for base in range(0, size, PIVOTS):
        home, at = base // 8, base % 8
        cols = [
            [jnp.broadcast_to(block[:, base + j : base + j + 1], (8, LANES)) for block in blocks]
            for j in range(PIVOTS)
        ]
        rows = [blocks[home][at + i : at + i + 1] for i in range(PIVOTS)]
        c = [[cols[j][home][at + i : at + i + 1] for j in range(PIVOTS)] for i in range(PIVOTS)]
        for i in range(PIVOTS):
            inverse = 1.0 / c[i][i]
            rows[i] = rows[i] * inverse
            for j in range(i + 1, PIVOTS):
                c[i][j] = c[i][j] * inverse
            for r in range(PIVOTS):
                if r != i:
                    f = c[r][i]
                    rows[r] = rows[r] - f * rows[i]
                    for j in range(i + 1, PIVOTS):
                        c[r][j] = c[r][j] - f * c[i][j]
        wide = [jnp.broadcast_to(row, (8, LANES)) for row in rows]
        for b in range(len(blocks)):
            new = blocks[b]
            for j in range(PIVOTS):
                new = new - cols[j][b] * wide[j]
            if b == home:
                for j in range(PIVOTS):
                    new = jnp.where(sub == at + j, wide[j], new)
            blocks[b] = new
    return jnp.concatenate(blocks, axis=0)


def update_kernel(
    lat_n,
    lon_n,
    state_ref,
    gather_ref,
    meta_ref,
    noise_ref,
    out_ref,
    x_ref,
):
    tile_lat, tile_lon, width = out_ref.shape
    pairs = width // LANES
    ilat = lax.axis_index("lat")
    ilon = lax.axis_index("lon")
    lon_cells = float(tile_lon * lon_n)
    count = meta_ref.shape[1]
    scale = 1.0 / (MEMBERS - 1)
    low_lanes = iota((count, LANES), 1) < MEMBERS

    table = meta_ref[...].T
    rows_of = [
        [meta_ref[8 * k + n : 8 * k + n + 1, :] for n in (0, 1, 6)] for k in range(BATCH_GROUPS)
    ]

    def col(k, n):
        return table[:, 8 * k + n : 8 * k + n + 1]

    def rho_of(lat_at, lon_at, k):
        glat, glon, inverse_radius = rows_of[k]
        dlat = jnp.abs(lat_at - glat)
        dlon = jnp.abs(lon_at - glon)
        dlon = jnp.minimum(dlon, lon_cells - dlon)
        return scale * taper(jnp.sqrt(dlat * dlat + dlon * dlon), inverse_radius)

    slots = gather_ref.shape[0]
    priors = []
    for k in range(BATCH_GROUPS):
        pick = jnp.where(iota((count, slots), 1).astype(jnp.float32) == col(k, 2), 1.0, 0.0)
        taken = pick_rows(pick.astype(jnp.bfloat16), gather_ref[...])
        turned = pltpu.roll(taken, MEMBERS, 1)
        odd = col(k, 3) > 0.5
        priors.append(jnp.where(odd != low_lanes, taken, turned))

    for k in range(BATCH_GROUPS):
        prior = priors[k]
        var = col(k, 5)
        inverse_var = 1.0 / var
        anom = prior - jnp.mean(prior, axis=1, keepdims=True)
        noise = jnp.concatenate([noise_ref[k], noise_ref[k]], axis=0).T
        rhs = col(k, 4) + jnp.sqrt(var) * noise - prior
        both = inverse_var * jnp.where(low_lanes, anom, rhs)
        aug = scale * dot3(dot_n, anom.T[:MEMBERS], both)
        aug += jnp.where(iota(aug.shape, 0) == iota(aug.shape, 1), 1.0, 0.0)
        solved = gauss_jordan(aug)
        solved = jnp.where(
            iota(solved.shape, 1) < MEMBERS, pltpu.roll(solved, MEMBERS, 1), solved
        )
        white = inverse_var * (rhs - dot3(dot_n, anom[:, :MEMBERS], solved))

        for later in range(k + 1, BATCH_GROUPS):
            cov = dot3(dot_t, priors[later][:, :MEMBERS], anom[:, :MEMBERS])
            cov = cov * rho_of(col(later, 0), col(later, 1), k)
            priors[later] = priors[later] + dot3(dot_n, cov, white)

        wide_anom = jnp.concatenate(
            [jnp.where(low_lanes, anom, 0.0), jnp.where(low_lanes, 0.0, anom)], axis=0
        )
        wide_white = jnp.concatenate(
            [jnp.where(low_lanes, white, 0.0), jnp.where(low_lanes, 0.0, white)], axis=0
        )
        rho = []
        for i in range(tile_lat):
            lat_at = (ilat * tile_lat + i).astype(jnp.float32)
            lon_at = (ilon * tile_lon + iota((tile_lon, 1), 0)).astype(jnp.float32)
            one = rho_of(lat_at, lon_at, k)
            rho.append(jnp.concatenate([one, one], axis=1)[None])
        rho = jnp.stack(rho, axis=0)

        x = state_ref[...] if k == 0 else x_ref[...]
        x_high, x_low = split(x)
        a_high, a_low = split(wide_anom)
        cov = dot_t(
            jnp.concatenate([x_high, x_low], axis=1), jnp.concatenate([a_high, a_high], axis=1)
        ) + dot_t(x_high, a_low)
        cov = cov.reshape(tile_lat, pairs, tile_lon, 2 * count) * rho
        cov = cov.reshape(tile_lat * pairs * tile_lon, 2 * count)
        c_high, c_low = split(cov)
        w_high, w_low = split(wide_white)
        two = dot_n(c_high, jnp.concatenate([w_high, w_low], axis=1))
        new = x + (two[:, :LANES] + two[:, LANES:] + dot_n(c_low, w_high))
        if k + 1 < BATCH_GROUPS:
            x_ref[...] = new
        else:
            for i in range(tile_lat):
                for p in range(pairs):
                    at = (i * pairs + p) * tile_lon
                    out_ref[i, :, p * LANES : (p + 1) * LANES] = new[at : at + tile_lon]


def body(
    ensemble,
    northward_wind,
    eastward_wind,
    spreading_strength,
    measurement_home_subdomain,
    obs_site,
    obs_class,
    cutoff_table,
    obs_value,
    obs_var,
    obs_noise,
):
    lat_n = lax.axis_size("lat")
    lon_n = lax.axis_size("lon")
    tile_lat, tile_lon, width = ensemble.shape
    rows = tile_lat * tile_lon * width // LANES
    count = obs_site.shape[1]
    vmem = pl.BlockSpec(memory_space=pltpu.VMEM)
    f32 = jnp.float32
    dma = pltpu.SemaphoreType.DMA
    loaded = (
        ensemble,
        spreading_strength,
        northward_wind,
        eastward_wind,
        measurement_home_subdomain,
        obs_site,
        obs_class,
        obs_value,
        obs_var,
        cutoff_table,
    )
    state, gathered, meta = pl.pallas_call(
        functools.partial(forecast_kernel, lat_n, lon_n),
        out_shape=(
            jax.ShapeDtypeStruct((rows, LANES), f32),
            jax.ShapeDtypeStruct((lat_n * lon_n * SLOT_ROWS, LANES), f32),
            jax.ShapeDtypeStruct((8 * BATCH_GROUPS, count), f32),
        ),
        in_specs=[vmem] * (len(loaded) - 1) + [pl.BlockSpec(memory_space=pltpu.SMEM)],
        out_specs=(vmem, vmem, vmem),
        scratch_shapes=[
            pltpu.VMEM((2, 2 * tile_lat, width), f32),
            pltpu.VMEM((4, 1, width), f32),
            pltpu.VMEM((3, tile_lat, tile_lon), f32),
            pltpu.VMEM((2, 2, tile_lon, width), f32),
            pltpu.VMEM((2, 2 * tile_lat, width), f32),
            pltpu.VMEM((4, 1, width), f32),
            pltpu.VMEM((4, 3, tile_lat, tile_lon), f32),
            pltpu.VMEM((lat_n, lon_n, SLOT_ROWS, LANES), f32),
            dma((12,)),
            dma((12,)),
            dma((lon_n - 1,)),
            dma((lon_n - 1,)),
            dma((lat_n - 1,)),
            dma((lat_n - 1,)),
        ],
        compiler_params=pltpu.CompilerParams(
            collective_id=0, has_side_effects=True, vmem_limit_bytes=32 << 20
        ),
    )(*loaded)
    return pl.pallas_call(
        functools.partial(update_kernel, lat_n, lon_n),
        out_shape=jax.ShapeDtypeStruct(ensemble.shape, f32),
        in_specs=[vmem] * 4,
        out_specs=vmem,
        scratch_shapes=[pltpu.VMEM((rows, LANES), f32)],
        compiler_params=pltpu.CompilerParams(vmem_limit_bytes=48 << 20),
    )(state, gathered, meta, jnp.swapaxes(obs_noise, 1, 2))


def solution(mesh):
    placed = (
        P("lat", "lon", None),
        P("lat", "lon"),
        P("lat", "lon"),
        P("lat", "lon"),
        P(),
        P(),
        P(),
        P(),
        P(),
        P(),
        P(),
    )
    return jax.shard_map(
        body, mesh=mesh, in_specs=placed, out_specs=P("lat", "lon", None), check_vma=False
    )
```

```python
import functools

import jax
import jax.numpy as jnp
from jax import lax
from jax.experimental import pallas as pl
from jax.experimental.pallas import tpu as pltpu
from jax.sharding import PartitionSpec as P

LEV = 28
MEMBERS = 64
BATCH_GROUPS = 3
CAP = 4
LANES = 128
PIVOTS = 4

advect_coef = 0.2
MESH = pl.DeviceIdType.MESH
SLOT_ROWS = -(-(BATCH_GROUPS * CAP) // 16) * 8


def floor_div(value, divisor):
    return jnp.floor((value + 0.5) * (1.0 / divisor))


def dot_t(a, b):
    return lax.dot_general(
        a, b, (((1,), (1,)), ((), ())), preferred_element_type=jnp.float32
    )


def dot_n(a, b):
    return lax.dot_general(
        a, b, (((1,), (0,)), ((), ())), preferred_element_type=jnp.float32
    )


def split(value):
    high = value.astype(jnp.bfloat16)
    low = (value - high.astype(jnp.float32)).astype(jnp.bfloat16)
    return high, low


def dot3(dot, a, b):
    a_high, a_low = split(a)
    b_high, b_low = split(b)
    return dot(a_high, b_high) + (dot(a_high, b_low) + dot(a_low, b_high))


def pick_rows(chosen, table):
    high, low = split(table)
    both = dot_n(chosen, jnp.concatenate([high, low], axis=1))
    return both[:, : table.shape[1]] + both[:, table.shape[1] :]


def iota(shape, dim):
    return lax.broadcasted_iota(jnp.int32, shape, dim)


def column(row):
    n = row.shape[1]
    return jnp.sum(
        jnp.where(iota((n, n), 0) == iota((n, n), 1), row, 0.0), axis=1, keepdims=True
    )


def forecast_kernel(
    lat_n,
    lon_n,
    ens_any,
    spread_any,
    north_any,
    east_any,
    owner_any,
    site_any,
    class_any,
    value_any,
    var_any,
    cutoff_any,
    state_ref,
    gather_ref,
    meta_ref,
    ens_ref,
    spread_ref,
    north_ref,
    east_ref,
    owner_ref,
    site_ref,
    class_ref,
    value_ref,
    var_ref,
    cutoff_ref,
    load_sem,
    edge,
    corner,
    wind,
    halo_lat,
    halo_lon,
    halo_corner,
    halo_wind,
    slots,
    send_sem,
    recv_sem,
    lon_send,
    lon_recv,
    lat_send,
    lat_recv,
):
    ilat = lax.axis_index("lat")
    ilon = lax.axis_index("lon")
    tile_lat, tile_lon, width = ens_ref.shape
    pairs = width // LANES
    lon_peers = [lax.rem(ilon + d, lon_n) for d in range(1, lon_n)]
    lat_peers = [lax.rem(ilat + d, lat_n) for d in range(1, lat_n)]

    up = lax.rem(ilat + 1, lat_n)
    down = lax.rem(ilat + lat_n - 1, lat_n)
    right = lax.rem(ilon + 1, lon_n)
    left = lax.rem(ilon + lon_n - 1, lon_n)
    diagonal = [(up, right), (up, left), (down, right), (down, left)]

    barrier = pltpu.get_barrier_semaphore()
    for peer in lon_peers:
        pl.semaphore_signal(barrier, inc=1, device_id=(ilat, peer), device_id_type=MESH)
    for peer in lat_peers:
        pl.semaphore_signal(barrier, inc=1, device_id=(peer, ilon), device_id_type=MESH)

    for device in diagonal:
        pl.semaphore_signal(barrier, inc=1, device_id=device, device_id_type=MESH)

    loads = []
    for n, (a, b) in enumerate(
        (
            (ens_any, ens_ref),
            (spread_any, spread_ref),
            (north_any, north_ref),
            (east_any, east_ref),
            (owner_any, owner_ref),
            (site_any, site_ref),
            (class_any, class_ref),
            (value_any, value_ref),
            (var_any, var_ref),
            (cutoff_any, cutoff_ref),
        )
    ):
        load = pltpu.make_async_copy(a, b, load_sem.at[n])
        load.start()
        loads.append(load)
    for load in loads:
        load.wait()

    top, end = tile_lat - 1, tile_lon - 1
    for i in range(tile_lat):
        for c in range(2):
            at = c * tile_lat + i
            edge[0, at : at + 1, :] = ens_ref[i, end - 1 + c : end + c, :]
            edge[1, at : at + 1, :] = ens_ref[i, c : c + 1, :]
    for n, (i, j) in enumerate(((top, end), (top, 0), (0, end), (0, 0))):
        corner[n] = ens_ref[i, j : j + 1, :]
    for n, ref in enumerate((spread_ref, north_ref, east_ref)):
        wind[n] = ref[...]

    pl.semaphore_wait(barrier, len(lon_peers) + len(lat_peers) + len(diagonal))
    first_tile, last_tile = ilat == 0, ilat == lat_n - 1
    moves = [
        (ens_ref.at[pl.ds(tile_lat - 2, 2)], halo_lat.at[0], (up, ilon), last_tile, first_tile),
        (ens_ref.at[pl.ds(0, 2)], halo_lat.at[1], (down, ilon), first_tile, last_tile),
        (edge.at[0], halo_lon.at[0], (ilat, right), None, None),
        (edge.at[1], halo_lon.at[1], (ilat, left), None, None),
        (wind, halo_wind.at[0], (up, ilon), last_tile, first_tile),
        (wind, halo_wind.at[1], (down, ilon), first_tile, last_tile),
        (wind, halo_wind.at[2], (ilat, right), None, None),
        (wind, halo_wind.at[3], (ilat, left), None, None),
        (corner.at[0], halo_corner.at[0], diagonal[0], last_tile, first_tile),
        (corner.at[1], halo_corner.at[1], diagonal[1], last_tile, first_tile),
        (corner.at[2], halo_corner.at[2], diagonal[2], first_tile, last_tile),
        (corner.at[3], halo_corner.at[3], diagonal[3], first_tile, last_tile),
    ]
    copies = []
    for n, (a, b, device, no_send, no_recv) in enumerate(moves):
        copy = pltpu.make_async_remote_copy(
            src_ref=a,
            dst_ref=b,
            send_sem=send_sem.at[n],
            recv_sem=recv_sem.at[n],
            device_id=device,
            device_id_type=MESH,
        )
        copies.append((copy, no_send, no_recv))
        if no_send is None:
            copy.start()
        else:
            pl.when(jnp.logical_not(no_send))(copy.start)

    same = iota((tile_lon, tile_lon), 0) == iota((tile_lon, tile_lon), 1)

    def weights(s, n, e):
        n = advect_coef * n
        e = advect_coef * e
        return (1.0 - 4.0 * s, s - n, s + n, s - e, s + e)

    def row_weights(rows):
        return weights(
            *(jnp.sum(jnp.where(same, row, 0.0), axis=1, keepdims=True) for row in rows)
        )

    coef = [
        row_weights([ref[i : i + 1, :] for ref in (spread_ref, north_ref, east_ref)])
        for i in range(tile_lat)
    ]

    count = owner_ref.shape[1]
    me = (ilat * lon_n + ilon).astype(jnp.float32)
    half = SLOT_ROWS
    slot_iota = iota((2 * half, count), 0)
    slot_id = (2 * (slot_iota % half) + slot_iota // half).astype(jnp.float32)
    slot_row = jnp.zeros((2 * half, 1), jnp.float32)
    slot_odd = jnp.zeros((2 * half, 1), jnp.float32)
    for k in range(BATCH_GROUPS):
        owner = owner_ref[k : k + 1, :].astype(jnp.float32)
        site = site_ref[k : k + 1, :].astype(jnp.float32)
        before = iota((count, count), 0) < iota((count, count), 1)
        earlier = (column(owner) == owner) & before
        rank = jnp.sum(jnp.where(earlier, 1.0, 0.0), axis=0, keepdims=True)
        cell = floor_div(site, LEV)
        level = site - LEV * cell
        cell_lat = floor_div(cell, tile_lon)
        cell_lon = cell - tile_lon * cell_lat
        pair = floor_div(level, 2)
        row = (cell_lat * pairs + pair) * tile_lon + cell_lon
        mine = (owner == me) & (slot_id == rank + float(CAP * k))
        slot_row += jnp.sum(jnp.where(mine, row, 0.0), axis=1, keepdims=True)
        slot_odd += jnp.sum(jnp.where(mine, level - 2.0 * pair, 0.0), axis=1, keepdims=True)
        tile_row = floor_div(owner, lon_n)
        radius = jnp.zeros((1, count), jnp.float32)
        for c in range(cutoff_ref.shape[0]):
            radius = jnp.where(
                class_ref[k : k + 1, :] == c, cutoff_ref[c].astype(jnp.float32), radius
            )
        slot = rank + float(CAP * k)
        slot_half = floor_div(slot, 2)
        meta = (
            tile_row * tile_lat + cell_lat,
            (owner - lon_n * tile_row) * tile_lon + cell_lon,
            owner * SLOT_ROWS + slot_half,
            slot - 2.0 * slot_half,
            value_ref[k : k + 1, :],
            var_ref[k : k + 1, :],
            1.0 / radius,
            jnp.zeros((1, count), jnp.float32),
        )
        meta_ref[8 * k : 8 * k + 8, :] = jnp.concatenate(meta, axis=0)
    rows = tile_lat * width // LANES * tile_lon
    pick = jnp.where(
        iota((2 * half, rows), 1).astype(jnp.float32) == slot_row, 1.0, 0.0
    ).astype(jnp.bfloat16)

    for copy, no_send, no_recv in copies:
        if no_send is None:
            copy.wait()
        else:
            pl.when(jnp.logical_not(no_send))(copy.wait_send)
            pl.when(jnp.logical_not(no_recv))(copy.wait_recv)

    def advance(weight, here, above, below, east, west):
        centre, c_n, c_s, c_e, c_w = weight
        return centre * here + c_n * above + c_s * below + c_e * east + c_w * west

    def along_row(weight, here, above, below, east_end, west_end):
        east = jnp.concatenate([here[1:], east_end], axis=0)
        west = jnp.concatenate([west_end, here[:-1]], axis=0)
        return advance(weight, here, above, below, east, west)

    below_1, below_2 = (jnp.where(first_tile, 0.0, halo_lat[0, n]) for n in (1, 0))
    above_1, above_2 = (jnp.where(last_tile, 0.0, halo_lat[1, n]) for n in (0, 1))
    corner_bw, corner_be = (jnp.where(first_tile, 0.0, halo_corner[n]) for n in (0, 1))
    corner_aw, corner_ae = (jnp.where(last_tile, 0.0, halo_corner[n]) for n in (2, 3))
    west_2, west_1 = halo_lon[0, :tile_lat], halo_lon[0, tile_lat:]
    east_1, east_2 = halo_lon[1, :tile_lat], halo_lon[1, tile_lat:]
    own_east, own_west = edge[0, tile_lat:], edge[1, :tile_lat]

    rows = [below_1] + [ens_ref[i] for i in range(tile_lat)] + [above_1]
    mid = [
        along_row(
            coef[i], rows[i + 1], rows[i + 2], rows[i], east_1[i : i + 1], west_1[i : i + 1]
        )
        for i in range(tile_lat)
    ]
    weight = row_weights([halo_wind[0, n, top : top + 1, :] for n in range(3)])
    mid_below = along_row(weight, below_1, rows[1], below_2, corner_be, corner_bw)
    weight = row_weights([halo_wind[1, n, 0:1, :] for n in range(3)])
    mid_above = along_row(weight, above_1, above_2, rows[tile_lat], corner_ae, corner_aw)
    mid_below = jnp.where(first_tile, 0.0, mid_below)
    mid_above = jnp.where(last_tile, 0.0, mid_above)

    def along_column(weight, here, above_end, below_end, east, west):
        above = jnp.concatenate([here[1:], above_end], axis=0)
        below = jnp.concatenate([below_end, here[:-1]], axis=0)
        return advance(weight, here, above, below, east, west)

    weight = weights(*(halo_wind[2, n, :, end : end + 1] for n in range(3)))
    mid_west = along_column(weight, west_1, corner_aw, corner_bw, own_west, west_2)
    weight = weights(*(halo_wind[3, n, :, 0:1] for n in range(3)))
    mid_east = along_column(weight, east_1, corner_ae, corner_be, east_2, own_east)

    rows = [mid_below] + mid + [mid_above]
    for i in range(tile_lat):
        new = along_row(
            coef[i], rows[i + 1], rows[i + 2], rows[i], mid_east[i : i + 1], mid_west[i : i + 1]
        )
        for p in range(pairs):
            at = (i * pairs + p) * tile_lon
            state_ref[at : at + tile_lon, :] = new[:, p * LANES : (p + 1) * LANES]

    taken = pick_rows(pick, state_ref[...])
    first, second = taken[:half], taken[half:]
    first = jnp.where(slot_odd[:half] < 0.5, first, pltpu.roll(first, MEMBERS, 1))
    second = jnp.where(slot_odd[half:] > 0.5, second, pltpu.roll(second, MEMBERS, 1))
    low_half = iota((half, LANES), 1) < MEMBERS
    slots[ilat, ilon] = jnp.where(low_half, first, second)

    def share(src_at, peers, sends, recvs, device_of):
        out = []
        for n, peer in enumerate(peers):
            copy = pltpu.make_async_remote_copy(
                src_ref=src_at,
                dst_ref=src_at,
                send_sem=sends.at[n],
                recv_sem=recvs.at[n],
                device_id=device_of(peer),
                device_id_type=MESH,
            )
            copy.start()
            out.append(copy)
        for copy in out:
            copy.wait()

    share(slots.at[ilat, ilon], lon_peers, lon_send, lon_recv, lambda peer: (ilat, peer))
    share(slots.at[ilat], lat_peers, lat_send, lat_recv, lambda peer: (peer, ilon))
    gather_ref[...] = slots[...].reshape(gather_ref.shape)


def taper(dist, inverse_radius):
    z = dist * inverse_radius
    inner = 1.0 + z * z * (-5.0 / 3.0 + z * (0.625 + z * (0.5 - 0.25 * z)))
    o = jnp.maximum(z, 1.0)
    outer = (
        4.0
        + o * (-5.0 + o * (5.0 / 3.0 + o * (0.625 + o * (-0.5 + o * (1.0 / 12.0)))))
        - (2.0 / 3.0) / o
    )
    return jnp.where(z <= 1.0, inner, jnp.where(z < 2.0, outer, 0.0))


def gauss_jordan(aug):
    size = aug.shape[0]
    blocks = [aug[i : i + 8] for i in range(0, size, 8)]
    sub = iota((8, LANES), 0)
    for base in range(0, size, PIVOTS):
        home, at = base // 8, base % 8
        cols = [
            [jnp.broadcast_to(block[:, base + j : base + j + 1], (8, LANES)) for block in blocks]
            for j in range(PIVOTS)
        ]
        rows = [blocks[home][at + i : at + i + 1] for i in range(PIVOTS)]
        c = [[cols[j][home][at + i : at + i + 1] for j in range(PIVOTS)] for i in range(PIVOTS)]
        for i in range(PIVOTS):
            inverse = 1.0 / c[i][i]
            rows[i] = rows[i] * inverse
            for j in range(i + 1, PIVOTS):
                c[i][j] = c[i][j] * inverse
            for r in range(PIVOTS):
                if r != i:
                    f = c[r][i]
                    rows[r] = rows[r] - f * rows[i]
                    for j in range(i + 1, PIVOTS):
                        c[r][j] = c[r][j] - f * c[i][j]
        wide = [jnp.broadcast_to(row, (8, LANES)) for row in rows]
        for b in range(len(blocks)):
            new = blocks[b]
            for j in range(PIVOTS):
                new = new - cols[j][b] * wide[j]
            if b == home:
                for j in range(PIVOTS):
                    new = jnp.where(sub == at + j, wide[j], new)
            blocks[b] = new
    return jnp.concatenate(blocks, axis=0)


def update_kernel(
    lat_n,
    lon_n,
    state_ref,
    gather_ref,
    meta_ref,
    noise_ref,
    out_ref,
    x_ref,
):
    tile_lat, tile_lon, width = out_ref.shape
    pairs = width // LANES
    ilat = lax.axis_index("lat")
    ilon = lax.axis_index("lon")
    lon_cells = float(tile_lon * lon_n)
    count = meta_ref.shape[1]
    scale = 1.0 / (MEMBERS - 1)
    low_lanes = iota((count, LANES), 1) < MEMBERS

    table = meta_ref[...].T
    rows_of = [
        [meta_ref[8 * k + n : 8 * k + n + 1, :] for n in (0, 1, 6)] for k in range(BATCH_GROUPS)
    ]

    def col(k, n):
        return table[:, 8 * k + n : 8 * k + n + 1]

    def rho_of(lat_at, lon_at, k):
        glat, glon, inverse_radius = rows_of[k]
        dlat = jnp.abs(lat_at - glat)
        dlon = jnp.abs(lon_at - glon)
        dlon = jnp.minimum(dlon, lon_cells - dlon)
        return scale * taper(jnp.sqrt(dlat * dlat + dlon * dlon), inverse_radius)

    slots = gather_ref.shape[0]
    priors = []
    for k in range(BATCH_GROUPS):
        pick = jnp.where(iota((count, slots), 1).astype(jnp.float32) == col(k, 2), 1.0, 0.0)
        taken = pick_rows(pick.astype(jnp.bfloat16), gather_ref[...])
        turned = pltpu.roll(taken, MEMBERS, 1)
        odd = col(k, 3) > 0.5
        priors.append(jnp.where(odd != low_lanes, taken, turned))

    for k in range(BATCH_GROUPS):
        prior = priors[k]
        var = col(k, 5)
        inverse_var = 1.0 / var
        anom = prior - jnp.mean(prior, axis=1, keepdims=True)
        noise = jnp.concatenate([noise_ref[k], noise_ref[k]], axis=0).T
        rhs = col(k, 4) + jnp.sqrt(var) * noise - prior
        both = inverse_var * jnp.where(low_lanes, anom, rhs)
        aug = scale * dot3(dot_n, anom.T[:MEMBERS], both)
        aug += jnp.where(iota(aug.shape, 0) == iota(aug.shape, 1), 1.0, 0.0)
        solved = gauss_jordan(aug)
        solved = jnp.where(
            iota(solved.shape, 1) < MEMBERS, pltpu.roll(solved, MEMBERS, 1), solved
        )
        white = inverse_var * (rhs - dot3(dot_n, anom[:, :MEMBERS], solved))

        for later in range(k + 1, BATCH_GROUPS):
            cov = dot3(dot_t, priors[later][:, :MEMBERS], anom[:, :MEMBERS])
            cov = cov * rho_of(col(later, 0), col(later, 1), k)
            priors[later] = priors[later] + dot3(dot_n, cov, white)

        wide_anom = jnp.concatenate(
            [jnp.where(low_lanes, anom, 0.0), jnp.where(low_lanes, 0.0, anom)], axis=0
        )
        wide_white = jnp.concatenate(
            [jnp.where(low_lanes, white, 0.0), jnp.where(low_lanes, 0.0, white)], axis=0
        )
        rho = []
        for i in range(tile_lat):
            lat_at = (ilat * tile_lat + i).astype(jnp.float32)
            lon_at = (ilon * tile_lon + iota((tile_lon, 1), 0)).astype(jnp.float32)
            one = rho_of(lat_at, lon_at, k)
            rho.append(jnp.concatenate([one, one], axis=1)[None])
        rho = jnp.stack(rho, axis=0)

        x = state_ref[...] if k == 0 else x_ref[...]
        x_high, x_low = split(x)
        a_high, a_low = split(wide_anom)
        cov = dot_t(
            jnp.concatenate([x_high, x_low], axis=1), jnp.concatenate([a_high, a_high], axis=1)
        ) + dot_t(x_high, a_low)
        cov = cov.reshape(tile_lat, pairs, tile_lon, 2 * count) * rho
        cov = cov.reshape(tile_lat * pairs * tile_lon, 2 * count)
        c_high, c_low = split(cov)
        w_high, w_low = split(wide_white)
        two = dot_n(c_high, jnp.concatenate([w_high, w_low], axis=1))
        new = x + (two[:, :LANES] + two[:, LANES:] + dot_n(c_low, w_high))
        if k + 1 < BATCH_GROUPS:
            x_ref[...] = new
        else:
            for i in range(tile_lat):
                for p in range(pairs):
                    at = (i * pairs + p) * tile_lon
                    out_ref[i, :, p * LANES : (p + 1) * LANES] = new[at : at + tile_lon]


def body(
    ensemble,
    northward_wind,
    eastward_wind,
    spreading_strength,
    measurement_home_subdomain,
    obs_site,
    obs_class,
    cutoff_table,
    obs_value,
    obs_var,
    obs_noise,
):
    lat_n = lax.axis_size("lat")
    lon_n = lax.axis_size("lon")
    tile_lat, tile_lon, width = ensemble.shape
    rows = tile_lat * tile_lon * width // LANES
    count = obs_site.shape[1]
    vmem = pl.BlockSpec(memory_space=pltpu.VMEM)
    f32 = jnp.float32
    dma = pltpu.SemaphoreType.DMA
    loaded = (
        ensemble,
        spreading_strength,
        northward_wind,
        eastward_wind,
        measurement_home_subdomain,
        obs_site,
        obs_class,
        obs_value,
        obs_var,
        cutoff_table,
    )
    state, gathered, meta = pl.pallas_call(
        functools.partial(forecast_kernel, lat_n, lon_n),
        out_shape=(
            jax.ShapeDtypeStruct((rows, LANES), f32),
            jax.ShapeDtypeStruct((lat_n * lon_n * SLOT_ROWS, LANES), f32),
            jax.ShapeDtypeStruct((8 * BATCH_GROUPS, count), f32),
        ),
        in_specs=[pl.BlockSpec(memory_space=pl.ANY)] * len(loaded),
        out_specs=(vmem, vmem, vmem),
        scratch_shapes=[pltpu.VMEM(a.shape, a.dtype) for a in loaded[:-1]]
        + [
            pltpu.SMEM(cutoff_table.shape, cutoff_table.dtype),
            dma((len(loaded),)),
            pltpu.VMEM((2, 2 * tile_lat, width), f32),
            pltpu.VMEM((4, 1, width), f32),
            pltpu.VMEM((3, tile_lat, tile_lon), f32),
            pltpu.VMEM((2, 2, tile_lon, width), f32),
            pltpu.VMEM((2, 2 * tile_lat, width), f32),
            pltpu.VMEM((4, 1, width), f32),
            pltpu.VMEM((4, 3, tile_lat, tile_lon), f32),
            pltpu.VMEM((lat_n, lon_n, SLOT_ROWS, LANES), f32),
            dma((12,)),
            dma((12,)),
            dma((lon_n - 1,)),
            dma((lon_n - 1,)),
            dma((lat_n - 1,)),
            dma((lat_n - 1,)),
        ],
        compiler_params=pltpu.CompilerParams(
            collective_id=0, has_side_effects=True, vmem_limit_bytes=63 << 20
        ),
    )(*loaded)
    return pl.pallas_call(
        functools.partial(update_kernel, lat_n, lon_n),
        out_shape=jax.ShapeDtypeStruct(ensemble.shape, f32),
        in_specs=[vmem] * 4,
        out_specs=vmem,
        scratch_shapes=[pltpu.VMEM((rows, LANES), f32)],
        compiler_params=pltpu.CompilerParams(vmem_limit_bytes=63 << 20),
    )(state, gathered, meta, jnp.swapaxes(obs_noise, 1, 2))


def solution(mesh):
    placed = (
        P("lat", "lon", None),
        P("lat", "lon"),
        P("lat", "lon"),
        P("lat", "lon"),
        P(),
        P(),
        P(),
        P(),
        P(),
        P(),
        P(),
    )
    return jax.shard_map(
        body, mesh=mesh, in_specs=placed, out_specs=P("lat", "lon", None), check_vma=False
    )
```

```python
import functools

import jax
import jax.numpy as jnp
from jax import lax
from jax.experimental import pallas as pl
from jax.experimental.pallas import tpu as pltpu
from jax.sharding import PartitionSpec as P

LEV = 28
MEMBERS = 64
BATCH_GROUPS = 3
CAP = 4
LANES = 128
PIVOTS = 8

advect_coef = 0.2
MESH = pl.DeviceIdType.MESH
SLOT_ROWS = -(-(BATCH_GROUPS * CAP) // 16) * 8


def floor_div(value, divisor):
    return jnp.floor((value + 0.5) * (1.0 / divisor))


def dot_t(a, b):
    return lax.dot_general(
        a, b, (((1,), (1,)), ((), ())), preferred_element_type=jnp.float32
    )


def dot_n(a, b):
    return lax.dot_general(
        a, b, (((1,), (0,)), ((), ())), preferred_element_type=jnp.float32
    )


def split(value):
    high = value.astype(jnp.bfloat16)
    low = (value - high.astype(jnp.float32)).astype(jnp.bfloat16)
    return high, low


def dot3(dot, a, b):
    a_high, a_low = split(a)
    b_high, b_low = split(b)
    return dot(a_high, b_high) + (dot(a_high, b_low) + dot(a_low, b_high))


def pick_rows(chosen, table):
    high, low = split(table)
    both = dot_n(chosen, jnp.concatenate([high, low], axis=1))
    return both[:, : table.shape[1]] + both[:, table.shape[1] :]


def iota(shape, dim):
    return lax.broadcasted_iota(jnp.int32, shape, dim)


def column(row):
    n = row.shape[1]
    return jnp.sum(
        jnp.where(iota((n, n), 0) == iota((n, n), 1), row, 0.0), axis=1, keepdims=True
    )


def forecast_kernel(
    lat_n,
    lon_n,
    ens_any,
    spread_any,
    north_any,
    east_any,
    owner_any,
    site_any,
    class_any,
    value_any,
    var_any,
    cutoff_any,
    state_ref,
    gather_ref,
    meta_ref,
    ens_ref,
    spread_ref,
    north_ref,
    east_ref,
    owner_ref,
    site_ref,
    class_ref,
    value_ref,
    var_ref,
    cutoff_ref,
    load_sem,
    edge,
    corner,
    wind,
    halo_lat,
    halo_lon,
    halo_corner,
    halo_wind,
    slots,
    send_sem,
    recv_sem,
    lon_send,
    lon_recv,
    lat_send,
    lat_recv,
):
    ilat = lax.axis_index("lat")
    ilon = lax.axis_index("lon")
    tile_lat, tile_lon, width = ens_ref.shape
    pairs = width // LANES
    lon_peers = [lax.rem(ilon + d, lon_n) for d in range(1, lon_n)]
    lat_peers = [lax.rem(ilat + d, lat_n) for d in range(1, lat_n)]

    up = lax.rem(ilat + 1, lat_n)
    down = lax.rem(ilat + lat_n - 1, lat_n)
    right = lax.rem(ilon + 1, lon_n)
    left = lax.rem(ilon + lon_n - 1, lon_n)
    diagonal = [(up, right), (up, left), (down, right), (down, left)]

    barrier = pltpu.get_barrier_semaphore()
    for peer in lon_peers:
        pl.semaphore_signal(barrier, inc=1, device_id=(ilat, peer), device_id_type=MESH)
    for peer in lat_peers:
        pl.semaphore_signal(barrier, inc=1, device_id=(peer, ilon), device_id_type=MESH)

    for device in diagonal:
        pl.semaphore_signal(barrier, inc=1, device_id=device, device_id_type=MESH)

    loads = []
    for n, (a, b) in enumerate(
        (
            (ens_any, ens_ref),
            (spread_any, spread_ref),
            (north_any, north_ref),
            (east_any, east_ref),
            (owner_any, owner_ref),
            (site_any, site_ref),
            (class_any, class_ref),
            (value_any, value_ref),
            (var_any, var_ref),
            (cutoff_any, cutoff_ref),
        )
    ):
        load = pltpu.make_async_copy(a, b, load_sem.at[n])
        load.start()
        loads.append(load)
    for load in loads:
        load.wait()

    top, end = tile_lat - 1, tile_lon - 1
    for i in range(tile_lat):
        for c in range(2):
            at = c * tile_lat + i
            edge[0, at : at + 1, :] = ens_ref[i, end - 1 + c : end + c, :]
            edge[1, at : at + 1, :] = ens_ref[i, c : c + 1, :]
    for n, (i, j) in enumerate(((top, end), (top, 0), (0, end), (0, 0))):
        corner[n] = ens_ref[i, j : j + 1, :]
    for n, ref in enumerate((spread_ref, north_ref, east_ref)):
        wind[n] = ref[...]

    pl.semaphore_wait(barrier, len(lon_peers) + len(lat_peers) + len(diagonal))
    first_tile, last_tile = ilat == 0, ilat == lat_n - 1
    moves = [
        (ens_ref.at[pl.ds(tile_lat - 2, 2)], halo_lat.at[0], (up, ilon), last_tile, first_tile),
        (ens_ref.at[pl.ds(0, 2)], halo_lat.at[1], (down, ilon), first_tile, last_tile),
        (edge.at[0], halo_lon.at[0], (ilat, right), None, None),
        (edge.at[1], halo_lon.at[1], (ilat, left), None, None),
        (wind, halo_wind.at[0], (up, ilon), last_tile, first_tile),
        (wind, halo_wind.at[1], (down, ilon), first_tile, last_tile),
        (wind, halo_wind.at[2], (ilat, right), None, None),
        (wind, halo_wind.at[3], (ilat, left), None, None),
        (corner.at[0], halo_corner.at[0], diagonal[0], last_tile, first_tile),
        (corner.at[1], halo_corner.at[1], diagonal[1], last_tile, first_tile),
        (corner.at[2], halo_corner.at[2], diagonal[2], first_tile, last_tile),
        (corner.at[3], halo_corner.at[3], diagonal[3], first_tile, last_tile),
    ]
    copies = []
    for n, (a, b, device, no_send, no_recv) in enumerate(moves):
        copy = pltpu.make_async_remote_copy(
            src_ref=a,
            dst_ref=b,
            send_sem=send_sem.at[n],
            recv_sem=recv_sem.at[n],
            device_id=device,
            device_id_type=MESH,
        )
        copies.append((copy, no_send, no_recv))
        if no_send is None:
            copy.start()
        else:
            pl.when(jnp.logical_not(no_send))(copy.start)

    same = iota((tile_lon, tile_lon), 0) == iota((tile_lon, tile_lon), 1)

    def weights(s, n, e):
        n = advect_coef * n
        e = advect_coef * e
        return (1.0 - 4.0 * s, s - n, s + n, s - e, s + e)

    def row_weights(rows):
        return weights(
            *(jnp.sum(jnp.where(same, row, 0.0), axis=1, keepdims=True) for row in rows)
        )

    coef = [
        row_weights([ref[i : i + 1, :] for ref in (spread_ref, north_ref, east_ref)])
        for i in range(tile_lat)
    ]

    count = owner_ref.shape[1]
    me = (ilat * lon_n + ilon).astype(jnp.float32)
    half = SLOT_ROWS
    slot_iota = iota((2 * half, count), 0)
    slot_id = (2 * (slot_iota % half) + slot_iota // half).astype(jnp.float32)
    slot_row = jnp.zeros((2 * half, 1), jnp.float32)
    slot_odd = jnp.zeros((2 * half, 1), jnp.float32)
    for k in range(BATCH_GROUPS):
        owner = owner_ref[k : k + 1, :].astype(jnp.float32)
        site = site_ref[k : k + 1, :].astype(jnp.float32)
        before = iota((count, count), 0) < iota((count, count), 1)
        earlier = (column(owner) == owner) & before
        rank = jnp.sum(jnp.where(earlier, 1.0, 0.0), axis=0, keepdims=True)
        cell = floor_div(site, LEV)
        level = site - LEV * cell
        cell_lat = floor_div(cell, tile_lon)
        cell_lon = cell - tile_lon * cell_lat
        pair = floor_div(level, 2)
        row = (cell_lat * pairs + pair) * tile_lon + cell_lon
        mine = (owner == me) & (slot_id == rank + float(CAP * k))
        slot_row += jnp.sum(jnp.where(mine, row, 0.0), axis=1, keepdims=True)
        slot_odd += jnp.sum(jnp.where(mine, level - 2.0 * pair, 0.0), axis=1, keepdims=True)
        tile_row = floor_div(owner, lon_n)
        radius = jnp.zeros((1, count), jnp.float32)
        for c in range(cutoff_ref.shape[0]):
            radius = jnp.where(
                class_ref[k : k + 1, :] == c, cutoff_ref[c].astype(jnp.float32), radius
            )
        slot = rank + float(CAP * k)
        slot_half = floor_div(slot, 2)
        meta = (
            tile_row * tile_lat + cell_lat,
            (owner - lon_n * tile_row) * tile_lon + cell_lon,
            owner * SLOT_ROWS + slot_half,
            slot - 2.0 * slot_half,
            value_ref[k : k + 1, :],
            var_ref[k : k + 1, :],
            1.0 / radius,
            jnp.zeros((1, count), jnp.float32),
        )
        meta_ref[8 * k : 8 * k + 8, :] = jnp.concatenate(meta, axis=0)
    rows = tile_lat * width // LANES * tile_lon
    pick = jnp.where(
        iota((2 * half, rows), 1).astype(jnp.float32) == slot_row, 1.0, 0.0
    ).astype(jnp.bfloat16)

    for copy, no_send, no_recv in copies:
        if no_send is None:
            copy.wait()
        else:
            pl.when(jnp.logical_not(no_send))(copy.wait_send)
            pl.when(jnp.logical_not(no_recv))(copy.wait_recv)

    def advance(weight, here, above, below, east, west):
        centre, c_n, c_s, c_e, c_w = weight
        return centre * here + c_n * above + c_s * below + c_e * east + c_w * west

    def along_row(weight, here, above, below, east_end, west_end):
        east = jnp.concatenate([here[1:], east_end], axis=0)
        west = jnp.concatenate([west_end, here[:-1]], axis=0)
        return advance(weight, here, above, below, east, west)

    below_1, below_2 = (jnp.where(first_tile, 0.0, halo_lat[0, n]) for n in (1, 0))
    above_1, above_2 = (jnp.where(last_tile, 0.0, halo_lat[1, n]) for n in (0, 1))
    corner_bw, corner_be = (jnp.where(first_tile, 0.0, halo_corner[n]) for n in (0, 1))
    corner_aw, corner_ae = (jnp.where(last_tile, 0.0, halo_corner[n]) for n in (2, 3))
    west_2, west_1 = halo_lon[0, :tile_lat], halo_lon[0, tile_lat:]
    east_1, east_2 = halo_lon[1, :tile_lat], halo_lon[1, tile_lat:]
    own_east, own_west = edge[0, tile_lat:], edge[1, :tile_lat]

    rows = [below_1] + [ens_ref[i] for i in range(tile_lat)] + [above_1]
    mid = [
        along_row(
            coef[i], rows[i + 1], rows[i + 2], rows[i], east_1[i : i + 1], west_1[i : i + 1]
        )
        for i in range(tile_lat)
    ]
    weight = row_weights([halo_wind[0, n, top : top + 1, :] for n in range(3)])
    mid_below = along_row(weight, below_1, rows[1], below_2, corner_be, corner_bw)
    weight = row_weights([halo_wind[1, n, 0:1, :] for n in range(3)])
    mid_above = along_row(weight, above_1, above_2, rows[tile_lat], corner_ae, corner_aw)
    mid_below = jnp.where(first_tile, 0.0, mid_below)
    mid_above = jnp.where(last_tile, 0.0, mid_above)

    def along_column(weight, here, above_end, below_end, east, west):
        above = jnp.concatenate([here[1:], above_end], axis=0)
        below = jnp.concatenate([below_end, here[:-1]], axis=0)
        return advance(weight, here, above, below, east, west)

    weight = weights(*(halo_wind[2, n, :, end : end + 1] for n in range(3)))
    mid_west = along_column(weight, west_1, corner_aw, corner_bw, own_west, west_2)
    weight = weights(*(halo_wind[3, n, :, 0:1] for n in range(3)))
    mid_east = along_column(weight, east_1, corner_ae, corner_be, east_2, own_east)

    rows = [mid_below] + mid + [mid_above]
    for i in range(tile_lat):
        new = along_row(
            coef[i], rows[i + 1], rows[i + 2], rows[i], mid_east[i : i + 1], mid_west[i : i + 1]
        )
        for p in range(pairs):
            at = (i * pairs + p) * tile_lon
            state_ref[at : at + tile_lon, :] = new[:, p * LANES : (p + 1) * LANES]

    taken = pick_rows(pick, state_ref[...])
    first, second = taken[:half], taken[half:]
    first = jnp.where(slot_odd[:half] < 0.5, first, pltpu.roll(first, MEMBERS, 1))
    second = jnp.where(slot_odd[half:] > 0.5, second, pltpu.roll(second, MEMBERS, 1))
    low_half = iota((half, LANES), 1) < MEMBERS
    slots[ilat, ilon] = jnp.where(low_half, first, second)

    def share(src_at, peers, sends, recvs, device_of):
        out = []
        for n, peer in enumerate(peers):
            copy = pltpu.make_async_remote_copy(
                src_ref=src_at,
                dst_ref=src_at,
                send_sem=sends.at[n],
                recv_sem=recvs.at[n],
                device_id=device_of(peer),
                device_id_type=MESH,
            )
            copy.start()
            out.append(copy)
        for copy in out:
            copy.wait()

    share(slots.at[ilat, ilon], lon_peers, lon_send, lon_recv, lambda peer: (ilat, peer))
    share(slots.at[ilat], lat_peers, lat_send, lat_recv, lambda peer: (peer, ilon))
    gather_ref[...] = slots[...].reshape(gather_ref.shape)


def taper(dist, inverse_radius):
    z = dist * inverse_radius
    inner = 1.0 + z * z * (-5.0 / 3.0 + z * (0.625 + z * (0.5 - 0.25 * z)))
    o = jnp.maximum(z, 1.0)
    outer = (
        4.0
        + o * (-5.0 + o * (5.0 / 3.0 + o * (0.625 + o * (-0.5 + o * (1.0 / 12.0)))))
        - (2.0 / 3.0) / o
    )
    return jnp.where(z <= 1.0, inner, jnp.where(z < 2.0, outer, 0.0))


def gauss_jordan(aug):
    size = aug.shape[0]
    blocks = [aug[i : i + 8] for i in range(0, size, 8)]
    sub = iota((8, LANES), 0)
    for base in range(0, size, PIVOTS):
        home, at = base // 8, base % 8
        cols = [
            [jnp.broadcast_to(block[:, base + j : base + j + 1], (8, LANES)) for block in blocks]
            for j in range(PIVOTS)
        ]
        rows = [blocks[home][at + i : at + i + 1] for i in range(PIVOTS)]
        c = [[cols[j][home][at + i : at + i + 1] for j in range(PIVOTS)] for i in range(PIVOTS)]
        for i in range(PIVOTS):
            inverse = 1.0 / c[i][i]
            rows[i] = rows[i] * inverse
            for j in range(i + 1, PIVOTS):
                c[i][j] = c[i][j] * inverse
            for r in range(PIVOTS):
                if r != i:
                    f = c[r][i]
                    rows[r] = rows[r] - f * rows[i]
                    for j in range(i + 1, PIVOTS):
                        c[r][j] = c[r][j] - f * c[i][j]
        wide = [jnp.broadcast_to(row, (8, LANES)) for row in rows]
        for b in range(len(blocks)):
            new = blocks[b]
            for j in range(PIVOTS):
                new = new - cols[j][b] * wide[j]
            if b == home:
                for j in range(PIVOTS):
                    new = jnp.where(sub == at + j, wide[j], new)
            blocks[b] = new
    return jnp.concatenate(blocks, axis=0)


def update_kernel(
    lat_n,
    lon_n,
    state_ref,
    gather_ref,
    meta_ref,
    noise_ref,
    out_ref,
    x_ref,
):
    tile_lat, tile_lon, width = out_ref.shape
    pairs = width // LANES
    ilat = lax.axis_index("lat")
    ilon = lax.axis_index("lon")
    lon_cells = float(tile_lon * lon_n)
    count = meta_ref.shape[1]
    scale = 1.0 / (MEMBERS - 1)
    low_lanes = iota((count, LANES), 1) < MEMBERS

    table = meta_ref[...].T
    rows_of = [
        [meta_ref[8 * k + n : 8 * k + n + 1, :] for n in (0, 1, 6)] for k in range(BATCH_GROUPS)
    ]

    def col(k, n):
        return table[:, 8 * k + n : 8 * k + n + 1]

    def rho_of(lat_at, lon_at, k):
        glat, glon, inverse_radius = rows_of[k]
        dlat = jnp.abs(lat_at - glat)
        dlon = jnp.abs(lon_at - glon)
        dlon = jnp.minimum(dlon, lon_cells - dlon)
        return scale * taper(jnp.sqrt(dlat * dlat + dlon * dlon), inverse_radius)

    slots = gather_ref.shape[0]
    priors = []
    for k in range(BATCH_GROUPS):
        pick = jnp.where(iota((count, slots), 1).astype(jnp.float32) == col(k, 2), 1.0, 0.0)
        taken = pick_rows(pick.astype(jnp.bfloat16), gather_ref[...])
        turned = pltpu.roll(taken, MEMBERS, 1)
        odd = col(k, 3) > 0.5
        priors.append(jnp.where(odd != low_lanes, taken, turned))

    for k in range(BATCH_GROUPS):
        prior = priors[k]
        var = col(k, 5)
        inverse_var = 1.0 / var
        anom = prior - jnp.mean(prior, axis=1, keepdims=True)
        noise = jnp.concatenate([noise_ref[k], noise_ref[k]], axis=0).T
        rhs = col(k, 4) + jnp.sqrt(var) * noise - prior
        both = inverse_var * jnp.where(low_lanes, anom, rhs)
        aug = scale * dot3(dot_n, anom.T[:MEMBERS], both)
        aug += jnp.where(iota(aug.shape, 0) == iota(aug.shape, 1), 1.0, 0.0)
        solved = gauss_jordan(aug)
        solved = jnp.where(
            iota(solved.shape, 1) < MEMBERS, pltpu.roll(solved, MEMBERS, 1), solved
        )
        white = inverse_var * (rhs - dot3(dot_n, anom[:, :MEMBERS], solved))

        for later in range(k + 1, BATCH_GROUPS):
            cov = dot3(dot_t, priors[later][:, :MEMBERS], anom[:, :MEMBERS])
            cov = cov * rho_of(col(later, 0), col(later, 1), k)
            priors[later] = priors[later] + dot3(dot_n, cov, white)

        wide_anom = jnp.concatenate(
            [jnp.where(low_lanes, anom, 0.0), jnp.where(low_lanes, 0.0, anom)], axis=0
        )
        wide_white = jnp.concatenate(
            [jnp.where(low_lanes, white, 0.0), jnp.where(low_lanes, 0.0, white)], axis=0
        )
        rho = []
        for i in range(tile_lat):
            lat_at = (ilat * tile_lat + i).astype(jnp.float32)
            lon_at = (ilon * tile_lon + iota((tile_lon, 1), 0)).astype(jnp.float32)
            one = rho_of(lat_at, lon_at, k)
            rho.append(jnp.concatenate([one, one], axis=1)[None])
        rho = jnp.stack(rho, axis=0)

        x = state_ref[...] if k == 0 else x_ref[...]
        x_high, x_low = split(x)
        a_high, a_low = split(wide_anom)
        cov = dot_t(
            jnp.concatenate([x_high, x_low], axis=1), jnp.concatenate([a_high, a_high], axis=1)
        ) + dot_t(x_high, a_low)
        cov = cov.reshape(tile_lat, pairs, tile_lon, 2 * count) * rho
        cov = cov.reshape(tile_lat * pairs * tile_lon, 2 * count)
        c_high, c_low = split(cov)
        w_high, w_low = split(wide_white)
        two = dot_n(c_high, jnp.concatenate([w_high, w_low], axis=1))
        new = x + (two[:, :LANES] + two[:, LANES:] + dot_n(c_low, w_high))
        if k + 1 < BATCH_GROUPS:
            x_ref[...] = new
        else:
            for i in range(tile_lat):
                for p in range(pairs):
                    at = (i * pairs + p) * tile_lon
                    out_ref[i, :, p * LANES : (p + 1) * LANES] = new[at : at + tile_lon]


def body(
    ensemble,
    northward_wind,
    eastward_wind,
    spreading_strength,
    measurement_home_subdomain,
    obs_site,
    obs_class,
    cutoff_table,
    obs_value,
    obs_var,
    obs_noise,
):
    lat_n = lax.axis_size("lat")
    lon_n = lax.axis_size("lon")
    tile_lat, tile_lon, width = ensemble.shape
    rows = tile_lat * tile_lon * width // LANES
    count = obs_site.shape[1]
    vmem = pl.BlockSpec(memory_space=pltpu.VMEM)
    f32 = jnp.float32
    dma = pltpu.SemaphoreType.DMA
    loaded = (
        ensemble,
        spreading_strength,
        northward_wind,
        eastward_wind,
        measurement_home_subdomain,
        obs_site,
        obs_class,
        obs_value,
        obs_var,
        cutoff_table,
    )
    state, gathered, meta = pl.pallas_call(
        functools.partial(forecast_kernel, lat_n, lon_n),
        out_shape=(
            jax.ShapeDtypeStruct((rows, LANES), f32),
            jax.ShapeDtypeStruct((lat_n * lon_n * SLOT_ROWS, LANES), f32),
            jax.ShapeDtypeStruct((8 * BATCH_GROUPS, count), f32),
        ),
        in_specs=[pl.BlockSpec(memory_space=pl.ANY)] * len(loaded),
        out_specs=(vmem, vmem, vmem),
        scratch_shapes=[pltpu.VMEM(a.shape, a.dtype) for a in loaded[:-1]]
        + [
            pltpu.SMEM(cutoff_table.shape, cutoff_table.dtype),
            dma((len(loaded),)),
            pltpu.VMEM((2, 2 * tile_lat, width), f32),
            pltpu.VMEM((4, 1, width), f32),
            pltpu.VMEM((3, tile_lat, tile_lon), f32),
            pltpu.VMEM((2, 2, tile_lon, width), f32),
            pltpu.VMEM((2, 2 * tile_lat, width), f32),
            pltpu.VMEM((4, 1, width), f32),
            pltpu.VMEM((4, 3, tile_lat, tile_lon), f32),
            pltpu.VMEM((lat_n, lon_n, SLOT_ROWS, LANES), f32),
            dma((12,)),
            dma((12,)),
            dma((lon_n - 1,)),
            dma((lon_n - 1,)),
            dma((lat_n - 1,)),
            dma((lat_n - 1,)),
        ],
        compiler_params=pltpu.CompilerParams(
            collective_id=0, has_side_effects=True, vmem_limit_bytes=63 << 20
        ),
    )(*loaded)
    return pl.pallas_call(
        functools.partial(update_kernel, lat_n, lon_n),
        out_shape=jax.ShapeDtypeStruct(ensemble.shape, f32),
        in_specs=[vmem] * 4,
        out_specs=vmem,
        scratch_shapes=[pltpu.VMEM((rows, LANES), f32)],
        compiler_params=pltpu.CompilerParams(vmem_limit_bytes=63 << 20),
    )(state, gathered, meta, jnp.swapaxes(obs_noise, 1, 2))


def solution(mesh):
    placed = (
        P("lat", "lon", None),
        P("lat", "lon"),
        P("lat", "lon"),
        P("lat", "lon"),
        P(),
        P(),
        P(),
        P(),
        P(),
        P(),
        P(),
    )
    return jax.shard_map(
        body, mesh=mesh, in_specs=placed, out_specs=P("lat", "lon", None), check_vma=False
    )
```
